256 devices in a mesh: dp: 16 (over x_lo, y, core), feat: 16 (over z, x_hi).
Axes of the slice: x: 4 (x_hi: 2, x_lo: 2; x = x_hi * 2 + x_lo), y: 4, z: 8, core: 2. Of those that a mesh axis runs over, the one named last changes fastest.
Arguments:
- z_one: bfloat16 [2048, 16384], P('dp', 'feat'), may hold values from -80 to 80
- z_two: bfloat16 [2048, 16384], P('dp', 'feat'), may hold values from -80 to 80
- hidden_in: bfloat16 [2048, 16384], P('feat', 'dp'), may hold values from -6 to 6
- grad_acc: float32 [16384, 16384], P('dp', 'feat'), may hold values from -6 to 6
- loss_scale: float32 [1], replicated, may hold values from 128 to 512
Outputs:
- grad_out: float32 [16384, 16384], P('dp', 'feat')
- loss_value: float32 [1], replicated
The draws below stay inside these ranges and needn't reach their ends.
All inputs are finite; a program needn't handle non-finite values.
Results may differ from the reference program's by a relative error of at most 0.0065.
Values may be sent and summed in bfloat16 or wider, within the bound.
A program may use at most 128 MiB of HBM per device.

```python
import math
import jax
import jax.numpy as jnp
from jax import lax

F = 16384
H = 16384
BATCH = 2048


def rough_field(first_key, shape):
    gauss = jax.random.normal(first_key, shape, jnp.float32)
    return gauss


def pair_fields(key):
    subkeys = jax.random.split(key, 13)
    shape = (BATCH, F)
    common = rough_field(subkeys[0], shape)
    jitter = jax.random.normal(subkeys[2], shape, jnp.float32)
    shared = rough_field(subkeys[8], (BATCH,))
    quarter = jnp.arange(F, dtype=jnp.int32) * 4 // F
    position = jnp.arange(F, dtype=jnp.float32) / F
    region_short = jnp.exp(jax.random.uniform(subkeys[10], (4,), jnp.float32, math.log(0.3), math.log(1.5)))
    base_short = jnp.exp(jax.random.uniform(subkeys[3], (F,), jnp.float32, math.log(0.03), math.log(0.3)))
    shortfall = base_short * jnp.take(region_short, quarter) * jnp.exp(0.5 * math.log(3.0) * position)
    kinship = 1.0 - shortfall
    region_load = jnp.exp(jax.random.uniform(subkeys[11], (2, 4), jnp.float32, math.log(0.08), math.log(0.4)))
    loads = jnp.take(region_load, quarter, axis=1) * jax.random.uniform(subkeys[12], (2, F), jnp.float32, 0.7, 1.3)
    rows_up = jnp.exp(math.log(3.0) * jnp.arange(BATCH, dtype=jnp.float32) / BATCH) * jnp.exp(jax.random.uniform(subkeys[4], (BATCH,), jnp.float32, -0.35, 0.35))
    scale_one = jnp.exp(jax.random.uniform(subkeys[5], (F,), jnp.float32, math.log(0.3), math.log(3.0)))
    scale_two = jnp.exp(jax.random.uniform(subkeys[6], (F,), jnp.float32, math.log(0.3), math.log(3.0)))
    offsets = jax.random.uniform(subkeys[7], (2, F), jnp.float32, -2.0, 2.0)
    base_one = loads[0][None, :] * shared[:, None] + jnp.sqrt(1.0 - loads[0] * loads[0])[None, :] * common
    mixed = kinship[None, :] * common + jnp.sqrt(1.0 - kinship * kinship)[None, :] * jitter
    base_two = loads[1][None, :] * shared[:, None] + jnp.sqrt(1.0 - loads[1] * loads[1])[None, :] * mixed
    first = rows_up[:, None] * scale_one[None, :] * base_one + offsets[0][None, :]
    second = rows_up[:, None] * scale_two[None, :] * base_two + offsets[1][None, :]
    return (jnp.clip(first, -80.0, 80.0), jnp.clip(second, -80.0, 80.0))


def draw_z_one(key, part):
    first, second = pair_fields(key)
    return first.astype(jnp.bfloat16)


def draw_z_two(key, part):
    first, second = pair_fields(key)
    return second.astype(jnp.bfloat16)


def block_levels(stream_key, shape, cuts, smallest, high):
    def one(dim, shards_of):
        steps = jax.random.uniform(jax.random.fold_in(jax.random.fold_in(stream_key, 6), dim), (shards_of,), jnp.float32, smallest / len(cuts), high / len(cuts))
        return jnp.repeat(jnp.exp(steps), shape[dim] // shards_of).reshape((-1,) + (1,) * (len(shape) - dim - 1))

    level = one(*cuts[0])
    for cut in cuts[1:]:
        level = level * one(*cut)
    return level


def normal_values(key, extent, deviation, bound, pieces=(), held_as=jnp.bfloat16):
    values = deviation * jax.random.normal(key, extent, jnp.float32)
    if pieces:
        values = values * block_levels(key, extent, pieces, -0.22, 0.18)
    return jnp.clip(values, -bound, bound).astype(held_as)


def setup_inputs(seed: int = 0) -> dict:
    key_of = jax.random.split(jax.random.key(seed), 6)
    z_one = draw_z_one(jax.random.fold_in(key_of[5], 71), 0)
    z_two = draw_z_two(jax.random.fold_in(key_of[5], 71), 0)
    hidden_in = normal_values(key_of[2], (BATCH, H), 1.0, 6.0, ((0, 16), (1, 16)))
    grad_acc = normal_values(key_of[3], (H, F), 1.0, 6.0, ((0, 16), (1, 16)), jnp.float32)
    loss_scale = jnp.clip(jnp.exp(jax.random.uniform(key_of[4], (1,), jnp.float32, math.log(128.0), math.log(512.0))), 128.0, 512.0)
    return {"z_one": z_one, "z_two": z_two, "hidden_in": hidden_in, "grad_acc": grad_acc, "loss_scale": loss_scale}


off_weight = 0.0051
eps = 1e-05

def standardize(raw):
    values = raw.astype(jnp.float32)
    centre = lax.optimization_barrier(jnp.mean(values, axis=0))
    spread = lax.optimization_barrier(jnp.mean((values - centre) ** 2, axis=0))
    inverse = lax.rsqrt(spread + eps)
    return (((values - centre) * inverse).astype(jnp.bfloat16), inverse)

def reference(z_one, z_two, hidden_in, grad_acc, loss_scale):
    normed_one, inverse_one = standardize(z_one)
    normed_two, unused_inv = standardize(z_two)
    batch = z_one.shape[0]
    width = z_one.shape[1]
    count = 16
    block = width // count
    factor = loss_scale[0] / batch
    columns = jnp.arange(width, dtype=jnp.int32)

    def one_block(index):
        start = (index * block).astype(jnp.int32)
        row_part = lax.dynamic_slice_in_dim(normed_one, start, block, 1)
        corr = lax.dot_general(row_part, normed_two, (((0,), (0,)), ((), ())), preferred_element_type=jnp.float32) / batch
        on_diag = (start + jnp.arange(block, dtype=jnp.int32))[:, None] == columns[None, :]
        partial_loss = jnp.sum(jnp.where(on_diag, (1.0 - corr) ** 2, off_weight * corr * corr))
        cotangent = (jnp.where(on_diag, -2.0 * (1.0 - corr), 2.0 * off_weight * corr) * factor).astype(jnp.bfloat16)
        grads = lax.dot_general(normed_two, cotangent, (((1,), (1,)), ((), ())), preferred_element_type=jnp.float32)
        return (partial_loss, grads)
    parts, grads = lax.map(one_block, jnp.arange(count, dtype=jnp.int32))
    grad_norm = jnp.transpose(grads, (1, 0, 2)).reshape(batch, width)
    loss_value = jnp.sum(parts) / width
    share = normed_one.astype(jnp.float32)
    mean_grad = lax.optimization_barrier(jnp.mean(grad_norm, axis=0))
    mean_cross = lax.optimization_barrier(jnp.mean(grad_norm * share, axis=0))
    grad_z = ((grad_norm - mean_grad - share * mean_cross) * inverse_one).astype(jnp.bfloat16)
    weight_grad = lax.dot_general(hidden_in, grad_z, (((0,), (0,)), ((), ())), preferred_element_type=jnp.float32)
    return (grad_acc + weight_grad, jnp.reshape(loss_value, (1,)))
```

```python
import jax
import jax.numpy as jnp
from jax import lax
from jax.sharding import PartitionSpec as P

off_weight = 0.0051
eps = 1e-05


def standardize(raw):
    values = raw.astype(jnp.float32)
    centre = jnp.mean(values, axis=0)
    spread = jnp.mean((values - centre) ** 2, axis=0)
    inverse = lax.rsqrt(spread + eps)
    return ((values - centre) * inverse).astype(jnp.bfloat16), inverse


def body(z_one, z_two, hidden_in, grad_acc, loss_scale):
    dp_count = lax.axis_size("dp")
    feat_count = lax.axis_size("feat")
    dp_index = lax.axis_index("dp")
    local_rows, local_cols = z_one.shape
    batch = local_rows * dp_count
    width = local_cols * feat_count
    two_all = lax.all_gather(z_two, "dp", axis=0, tiled=True)
    one_all = lax.all_gather(z_one, "dp", axis=0, tiled=True)
    hidden_all = lax.all_gather(hidden_in, "feat", axis=0, tiled=True)
    normed_two, _ = standardize(two_all)
    normed_one, inverse_one = standardize(one_all)
    own_two = lax.dynamic_slice_in_dim(normed_two, dp_index * local_rows, local_rows, 0)
    own_one = lax.dynamic_slice_in_dim(normed_one, dp_index * local_rows, local_rows, 0)
    gram = lax.psum(
        lax.dot_general(
            own_two, normed_two, (((1,), (1,)), ((), ())), preferred_element_type=jnp.float32
        ),
        "feat",
    ).astype(jnp.bfloat16)
    spread = lax.dot_general(
        gram, normed_one, (((1,), (0,)), ((), ())), preferred_element_type=jnp.float32
    )
    corr_diag = (
        jnp.sum(normed_one.astype(jnp.float32) * normed_two.astype(jnp.float32), axis=0) / batch
    )
    share = own_one.astype(jnp.float32)
    scale = loss_scale[0] / batch
    weight_diag = scale * (-2.0 * (1.0 - corr_diag) - 2.0 * off_weight * corr_diag)
    grad_norm = spread * (scale * 2.0 * off_weight / batch) + own_two.astype(
        jnp.float32
    ) * weight_diag
    square_total = jnp.sum(spread * share) / (float(batch) * float(batch))
    diag_part = jnp.sum((1.0 - corr_diag) ** 2 - off_weight * corr_diag * corr_diag)
    loss_total = (
        lax.psum(off_weight * square_total + diag_part / dp_count, ("dp", "feat")) / width
    )
    sum_grad, sum_cross = lax.psum(
        (jnp.sum(grad_norm, axis=0), jnp.sum(grad_norm * share, axis=0)), "dp"
    )
    grad_z = (
        (grad_norm - sum_grad / batch - share * (sum_cross / batch)) * inverse_one
    ).astype(jnp.bfloat16)
    weight_grad = lax.dot_general(
        hidden_all,
        lax.all_gather(grad_z, "dp", axis=0, tiled=True),
        (((0,), (0,)), ((), ())),
        preferred_element_type=jnp.float32,
    )
    return (grad_acc + weight_grad, jnp.reshape(loss_total, (1,)))


def solution(mesh):
    placed = (P("dp", "feat"), P("dp", "feat"), P("feat", "dp"), P("dp", "feat"), P())
    return jax.shard_map(
        body, mesh=mesh, in_specs=placed, out_specs=(P("dp", "feat"), P()), check_vma=False
    )
```

```python
import functools

import jax
import jax.numpy as jnp
from jax import lax
from jax.experimental import pallas as pl
from jax.experimental.pallas import tpu as pltpu
from jax.sharding import PartitionSpec as P

MESH = pl.DeviceIdType.MESH
BF = jnp.bfloat16
F32 = jnp.float32
off_weight = 0.0051
eps = 1e-05
PEERS = 16
ROWS = 128
COLS = 1024
HALF = ROWS // 2
CHUNK = 32


def remote(src, dst, ss, rs, device):
    return pltpu.make_async_remote_copy(
        src_ref=src, dst_ref=dst, send_sem=ss, recv_sem=rs, device_id=device, device_id_type=MESH
    )


class DpGather:
    def __init__(self, buf, ss, rs, dp):
        self.buf, self.ss, self.rs = buf, ss, rs
        core, y, x = dp % 2, (dp // 2) % 4, dp // 8

        def block(x_, y_):
            return (x_ * 4 + y_) * 2 + core

        low, high, far = (y + 3) % 4, (y + 1) % 4, (y + 2) % 4
        self.own, self.ym, self.yp, self.y2 = (block(x, v) for v in (y, low, high, far))
        self.xo, self.xm, self.xp, self.x2 = (block(1 - x, v) for v in (y, low, high, far))
        self.flip = 1 - 2 * core
        self.table = {
            0: (self.own, None, self.yp, self.ym),
            1: (self.own, None, self.ym, self.yp),
            2: (self.own, None, self.xo, self.xo),
            3: (self.own, None, None, self.own),
            4: (self.ym, 0, self.yp, self.y2),
            5: (self.yp, 1, self.ym, self.y2),
            6: (self.ym, 1, self.xo, self.xm),
            7: (self.yp, 0, self.xo, self.xp),
            8: (self.xo, 0, self.yp, self.xm),
            9: (self.xo, 1, self.ym, self.xp),
            10: (self.ym, None, None, self.ym),
            11: (self.yp, None, None, self.yp),
            12: (self.xo, None, None, self.xo),
            13: (self.y2, None, self.xo, self.x2),
            14: (self.y2, None, None, self.y2),
            15: (self.xm, None, None, self.xm),
            16: (self.xp, None, None, self.xp),
            17: (self.x2, None, None, self.x2),
        }

    def ref(self, block, half):
        if half is None:
            return self.buf.at[block]
        return self.buf.at[block, pl.ds(half * HALF, HALF)]

    def copy(self, slot, received):
        sent, half, target, incoming = self.table[slot]
        if target is None:
            target = self.own + self.flip
            incoming = incoming + self.flip
        ref = self.ref(incoming if received else sent, half)
        return remote(ref, ref, self.ss.at[slot], self.rs.at[slot], {"dp": target})

    def send(self, *slots):
        for slot in slots:
            self.copy(slot, False).start()

    def recv(self, *slots):
        for slot in slots:
            self.copy(slot, True).wait_recv()

    def stage_a(self):
        self.send(0, 1, 2, 3)

    def stage_b(self):
        self.recv(0)
        self.send(4, 6, 10)
        self.recv(1)
        self.send(5, 7, 11)
        self.recv(2)
        self.send(8, 9, 12)

    def stage_c(self):
        self.recv(4, 5)
        self.send(13, 14)
        self.recv(6, 8)
        self.send(15)
        self.recv(7, 9)
        self.send(16)
        self.recv(13)
        self.send(17)

    def drain(self):
        for slot in range(18):
            self.copy(slot, False).wait_send()


class HiddenGather:
    def __init__(self, buf, ss, rs, feat):
        self.buf, self.ss, self.rs = buf, ss, rs
        z, xh = feat // 2, feat % 2
        self.rows = buf.shape[1] // 2

        def at(step, q):
            return ((z + 8 + step) % 8) * 2 + (xh if q == 0 else 1 - xh)

        up, down, partner = at(1, 0), at(-1, 0), at(0, 1)
        self.table = {0: (at(0, 0), None, partner, partner)}
        for q in range(2):
            base = 1 + 8 * q
            for k in range(4):
                last = k == 3
                self.table[base + 2 * k] = (at(-k, q), 0 if last else None, up, at(-k - 1, q))
                self.table[base + 2 * k + 1] = (at(k, q), 1 if last else None, down, at(k + 1, q))

    def copy(self, slot, received):
        sent, half, target, incoming = self.table[slot]
        block = incoming if received else sent
        if half is None:
            ref = self.buf.at[block]
        else:
            ref = self.buf.at[block, pl.ds(half * self.rows, self.rows)]
        return remote(ref, ref, self.ss.at[slot], self.rs.at[slot], {"feat": target})

    def send(self, *slots):
        for slot in slots:
            self.copy(slot, False).start()

    def recv(self, *slots):
        for slot in slots:
            self.copy(slot, True).wait_recv()

    def step(self, q, k):
        base = 1 + 8 * q + 2 * k
        if k:
            self.recv(base - 2, base - 1)
        self.send(base, base + 1)

    def drain(self):
        for slot in range(17):
            self.copy(slot, False).wait_send()


def exchange(axis, me, source, dst, ss, rs):
    def each(act):
        def step(j, carry):
            peer = (me + j) % PEERS
            act(peer)
            return carry

        lax.fori_loop(1, PEERS, step, 0)

    def start():
        each(
            lambda p: remote(source(p), dst.at[me], ss.at[p], rs.at[me], {axis: p}).start()
        )

    def wait_recv():
        each(
            lambda p: remote(source(p), dst.at[p], ss.at[p], rs.at[p], {axis: p}).wait_recv()
        )

    def wait_send():
        each(
            lambda p: remote(source(p), dst.at[me], ss.at[p], rs.at[me], {axis: p}).wait_send()
        )

    return start, wait_recv, wait_send


def over_rows(step, init):
    per = ROWS // CHUNK

    def body(i, carry):
        return step(i // per, pl.ds(pl.multiple_of((i % per) * CHUNK, CHUNK), CHUNK), carry)

    return lax.fori_loop(0, PEERS * per, body, init)


def fold(values):
    return jnp.sum(values.reshape(CHUNK // 8, 8, COLS), axis=0)


def statistics(buf, batch):
    zero = jnp.zeros((8, COLS), F32)

    def add(block, rows, acc):
        return acc + fold(buf[block, rows].astype(F32))

    centre = jnp.sum(over_rows(add, zero), axis=0, keepdims=True) / batch

    def add_square(block, rows, acc):
        off = buf[block, rows].astype(F32) - centre
        return acc + fold(off * off)

    spread = jnp.sum(over_rows(add_square, zero), axis=0, keepdims=True) / batch
    return centre, lax.rsqrt(spread + eps)


def kernel(
    z_one, z_two, hidden, scale_ref,
    weight, loss_ref,
    one, two, grad, hid, raw, part, part_in, gram, spread, sums, losses,
    local_sem, one_s, one_r, two_s, two_r, grad_s, grad_r, hid_s, hid_r,
    part_s, part_r, gram_s, gram_r, sums_s, sums_r, loss_s, loss_r,
):
    dp, feat = lax.axis_index("dp"), lax.axis_index("feat")
    batch = ROWS * PEERS
    width = COLS * PEERS

    local = [
        pltpu.make_async_copy(z_two, two.at[dp], local_sem.at[0]),
        pltpu.make_async_copy(z_one, one.at[dp], local_sem.at[1]),
        pltpu.make_async_copy(hidden, raw, local_sem.at[2]),
    ]
    for copy in local:
        copy.start()

    barrier = pltpu.get_barrier_semaphore()

    def greet(j, carry):
        pl.semaphore_signal(
            barrier, inc=1, device_id={"dp": (dp + j) % PEERS}, device_id_type=MESH
        )
        pl.semaphore_signal(
            barrier, inc=1, device_id={"feat": (feat + j) % PEERS}, device_id_type=MESH
        )
        return carry

    lax.fori_loop(1, PEERS, greet, 0)
    for copy in local:
        copy.wait()
    pl.semaphore_wait(barrier, 2 * (PEERS - 1))

    gather_two = DpGather(two, two_s, two_r, dp)
    gather_one = DpGather(one, one_s, one_r, dp)
    gather_grad = DpGather(grad, grad_s, grad_r, dp)
    gather_hid = HiddenGather(hid, hid_s, hid_r, feat)

    gather_two.stage_a()
    hid[feat] = raw[...].T
    gather_hid.send(0)
    gather_hid.step(0, 0)
    gather_two.stage_b()
    gather_one.stage_a()
    gather_hid.recv(0)
    gather_hid.step(1, 0)
    gather_two.stage_c()
    gather_hid.step(0, 1)
    gather_two.recv(3, 10, 11, 12, 14, 15, 16, 17)
    gather_two.drain()

    centre, inverse = statistics(two, batch)

    def norm_two(block, rows, carry):
        two[block, rows] = ((two[block, rows].astype(F32) - centre) * inverse).astype(BF)
        return carry

    over_rows(norm_two, 0)

    def gram_tiles(j, carry):
        pair = two[pl.ds(2 * j, 2)].reshape(2 * ROWS, COLS)
        tile = lax.dot_general(
            two[dp], pair, (((1,), (1,)), ((), ())), preferred_element_type=F32
        ).astype(BF)
        part[2 * j] = tile[:, :ROWS]
        part[2 * j + 1] = tile[:, ROWS:]
        return carry

    lax.fori_loop(0, PEERS // 2, gram_tiles, 0)
    part_start, part_recv, part_send = exchange(
        "feat", feat, lambda p: part.at[p], part_in, part_s, part_r
    )
    part_start()
    gather_one.stage_b()
    gather_hid.step(1, 1)
    part_in[feat] = part[feat]
    part_recv()

    def add_part(j, acc):
        return acc + part_in[j].astype(F32)

    gram[feat] = lax.fori_loop(0, PEERS, add_part, jnp.zeros((ROWS, ROWS), F32)).astype(BF)
    gram_start, gram_recv, gram_send = exchange(
        "feat", feat, lambda p: gram.at[feat], gram, gram_s, gram_r
    )
    gram_start()
    gather_one.stage_c()
    gather_one.recv(3, 10, 11, 12, 14, 15, 16, 17)
    gather_one.drain()

    centre_one, inverse_one = statistics(one, batch)

    def norm_one(block, rows, acc):
        normed = ((one[block, rows].astype(F32) - centre_one) * inverse_one).astype(BF)
        one[block, rows] = normed
        return acc + fold(normed.astype(F32) * two[block, rows].astype(F32))

    corr = (
        jnp.sum(over_rows(norm_one, jnp.zeros((8, COLS), F32)), axis=0, keepdims=True) / batch
    )
    scale = scale_ref[0] / batch
    weight_diag = scale * (-2.0 * (1.0 - corr) - 2.0 * off_weight * corr)

    gather_hid.step(0, 2)
    gram_recv()
    gather_hid.step(1, 2)

    spread[...] = jnp.zeros_like(spread)

    def spread_step(j, carry):
        rows = jnp.concatenate([gram[2 * j], gram[2 * j + 1]], axis=1)
        spread[...] += jnp.dot(
            rows, one[pl.ds(2 * j, 2)].reshape(2 * ROWS, COLS), preferred_element_type=F32
        )
        return carry

    lax.fori_loop(0, PEERS // 2, spread_step, 0)
    factor = scale * (2.0 * off_weight / batch)
    zero = jnp.zeros((8, COLS), F32)

    def norm_step(i, accs):
        rows = pl.ds(pl.multiple_of(i * CHUNK, CHUNK), CHUNK)
        raw_spread = spread[rows]
        share = one[dp, rows].astype(F32)
        value = raw_spread * factor + two[dp, rows].astype(F32) * weight_diag
        spread[rows] = value
        return (
            accs[0] + fold(value),
            accs[1] + fold(value * share),
            accs[2] + fold(raw_spread * share),
        )

    accs = lax.fori_loop(0, ROWS // CHUNK, norm_step, (zero, zero, zero))
    square = jnp.sum(accs[2], axis=0, keepdims=True) / (float(batch) * float(batch))
    terms = off_weight * square + (
        (1.0 - corr) * (1.0 - corr) - off_weight * corr * corr
    ) * (1.0 / PEERS)
    lanes = terms[:, :128]
    for k in range(1, COLS // 128):
        lanes = lanes + terms[:, k * 128 : (k + 1) * 128]
    sums[dp, 0:1, :COLS] = jnp.sum(accs[0], axis=0, keepdims=True)
    sums[dp, 1:2, :COLS] = jnp.sum(accs[1], axis=0, keepdims=True)
    sums[dp, 0:1, COLS:] = lanes
    sums[dp, 1:2, COLS:] = jnp.zeros_like(lanes)
    sums_start, sums_recv, sums_send = exchange(
        "dp", dp, lambda p: sums.at[dp], sums, sums_s, sums_r
    )
    sums_start()
    sums_recv()

    total = lax.fori_loop(
        0, PEERS, lambda j, acc: acc + sums[j], jnp.zeros((2, COLS + 128), F32)
    )
    mean_grad = total[0:1, :COLS] / batch
    mean_cross = total[1:2, :COLS] / batch

    def grad_step(i, carry):
        rows = pl.ds(pl.multiple_of(i * CHUNK, CHUNK), CHUNK)
        share = one[dp, rows].astype(F32)
        grad[dp, rows] = ((spread[rows] - mean_grad - share * mean_cross) * inverse_one).astype(BF)
        return carry

    lax.fori_loop(0, ROWS // CHUNK, grad_step, 0)
    gather_grad.stage_a()
    losses[feat] = total[:, COLS:]
    loss_start, loss_recv, loss_send = exchange(
        "feat", feat, lambda p: losses.at[feat], losses, loss_s, loss_r
    )
    loss_start()
    gather_hid.step(0, 3)
    gather_hid.step(1, 3)
    weight[...] = jnp.zeros_like(weight)
    gather_grad.stage_b()
    gather_hid.recv(7, 8, 15, 16)

    def add_pair(block):
        pair = block // 2
        rhs = grad[pl.ds(2 * pair, 2)].reshape(2 * ROWS, COLS)

        def step(i, carry):
            rows = pl.ds(pl.multiple_of(i * 256, 256), 256)
            lhs = jnp.concatenate([hid[2 * pair, rows], hid[2 * pair + 1, rows]], axis=1)
            weight[rows] += jnp.dot(lhs, rhs, preferred_element_type=F32)
            return carry

        lax.fori_loop(0, COLS // 256, step, 0)

    gather_grad.recv(3)
    add_pair(gather_grad.own)
    gather_grad.recv(10)
    add_pair(gather_grad.ym)
    gather_grad.stage_c()
    gather_grad.recv(11)
    add_pair(gather_grad.yp)
    gather_grad.recv(12)
    add_pair(gather_grad.xo)
    gather_grad.recv(14)
    add_pair(gather_grad.y2)
    gather_grad.recv(15)
    add_pair(gather_grad.xm)
    gather_grad.recv(16)
    add_pair(gather_grad.xp)
    gather_grad.recv(17)
    add_pair(gather_grad.x2)

    loss_recv()
    all_loss = lax.fori_loop(
        0, PEERS, lambda j, acc: acc + losses[j], jnp.zeros((2, 128), F32)
    )
    loss_ref[...] = jnp.broadcast_to(
        jnp.sum(all_loss, axis=(0, 1), keepdims=True) / width, loss_ref.shape
    )
    part_send()
    gram_send()
    sums_send()
    loss_send()
    gather_grad.drain()
    gather_hid.drain()


def body(z_one, z_two, hidden_in, grad_acc, loss_scale):
    any_space = pl.BlockSpec(memory_space=pl.ANY)
    dma = pltpu.SemaphoreType.DMA
    weight_grad, loss = pl.pallas_call(
        kernel,
        out_shape=(
            jax.ShapeDtypeStruct((COLS, COLS), F32),
            jax.ShapeDtypeStruct((8, 128), F32),
        ),
        in_specs=[any_space] * 3 + [pl.BlockSpec(memory_space=pltpu.SMEM)],
        out_specs=(
            pl.BlockSpec(memory_space=pltpu.VMEM),
            pl.BlockSpec(memory_space=pltpu.VMEM),
        ),
        scratch_shapes=[
            pltpu.VMEM((PEERS, ROWS, COLS), BF),
            pltpu.VMEM((PEERS, ROWS, COLS), BF),
            pltpu.VMEM((PEERS, ROWS, COLS), BF),
            pltpu.VMEM((PEERS, COLS, ROWS), BF),
            pltpu.VMEM((ROWS, COLS), BF),
            pltpu.VMEM((PEERS, ROWS, ROWS), BF),
            pltpu.VMEM((PEERS, ROWS, ROWS), BF),
            pltpu.VMEM((PEERS, ROWS, ROWS), BF),
            pltpu.VMEM((ROWS, COLS), F32),
            pltpu.VMEM((PEERS, 2, COLS + 128), F32),
            pltpu.VMEM((PEERS, 2, 128), F32),
            dma((3,)),
        ]
        + [dma((18,))] * 6
        + [dma((17,))] * 2
        + [dma((PEERS,))] * 8,
        compiler_params=pltpu.CompilerParams(
            collective_id=0, has_side_effects=True, vmem_limit_bytes=48 << 20
        ),
        cost_estimate=pl.CostEstimate(
            flops=6 * 10**9, bytes_accessed=8 * 10**6, transcendentals=0
        ),
        name="barlow",
    )(z_one, z_two, hidden_in, loss_scale)
    return grad_acc + weight_grad, loss[0, :1]


def solution(mesh):
    placed = (P("dp", "feat"), P("dp", "feat"), P("feat", "dp"), P("dp", "feat"), P())
    return jax.shard_map(
        body, mesh=mesh, in_specs=placed, out_specs=(P("dp", "feat"), P()), check_vma=False
    )
```

```python
import jax
import jax.numpy as jnp
from jax import lax
from jax.experimental import pallas as pl
from jax.experimental.pallas import tpu as pltpu
from jax.sharding import PartitionSpec as P

MESH = pl.DeviceIdType.MESH
BF = jnp.bfloat16
F32 = jnp.float32
off_weight = 0.0051
eps = 1e-05
PEERS = 16
ROWS = 128
COLS = 1024
HALF = ROWS // 2
CHUNK = 64


def remote(src, dst, ss, rs, device):
    return pltpu.make_async_remote_copy(
        src_ref=src, dst_ref=dst, send_sem=ss, recv_sem=rs, device_id=device, device_id_type=MESH
    )


class DpGather:
    def __init__(self, buf, ss, rs, dp):
        self.buf, self.ss, self.rs = buf, ss, rs
        core, y, x = dp % 2, (dp // 2) % 4, dp // 8

        def block(x_, y_):
            return (x_ * 4 + y_) * 2 + core

        low, high, far = (y + 3) % 4, (y + 1) % 4, (y + 2) % 4
        self.own, self.ym, self.yp, self.y2 = (block(x, v) for v in (y, low, high, far))
        self.xo, self.xm, self.xp, self.x2 = (block(1 - x, v) for v in (y, low, high, far))
        self.flip = 1 - 2 * core
        self.any_peer = {"dp": self.xo}
        self.table = [
            (self.own, 0, self.yp, self.ym),
            (self.own, 1, self.yp, self.ym),
            (self.own, 1, self.ym, self.yp),
            (self.own, 0, self.ym, self.yp),
            (self.own, None, self.xo, self.xo),
            (self.own, None, None, self.own),
            (self.ym, 0, self.yp, self.y2),
            (self.yp, 1, self.ym, self.y2),
            (self.xo, None, self.yp, self.xm),
            (self.xo, None, self.ym, self.xp),
            (self.y2, 0, self.xo, self.x2),
            (self.y2, 1, self.xo, self.x2),
            (self.ym, None, None, self.ym),
            (self.yp, None, None, self.yp),
            (self.xo, None, None, self.xo),
            (self.y2, None, None, self.y2),
            (self.xm, None, None, self.xm),
            (self.xp, None, None, self.xp),
            (self.x2, None, None, self.x2),
        ]
        self.near = [(v // 2, slot) for v, slot in ((self.own, 5), (self.xo, 14), (self.ym, 12), (self.yp, 13))]
        self.later = [(v // 2, slot) for v, slot in ((self.y2, 15), (self.xm, 16), (self.xp, 17), (self.x2, 18))]

    def copy(self, slot, received):
        sent, half, target, incoming = self.table[slot]
        if target is None:
            target = self.own + self.flip
            incoming = incoming + self.flip
        block = incoming if received else sent
        ref = self.buf.at[block]
        if half is not None:
            ref = self.buf.at[block, pl.ds(half * HALF, HALF)]
        return remote(ref, ref, self.ss, self.rs.at[slot], {"dp": target})

    def send(self, *slots):
        for slot in slots:
            self.copy(slot, False).start()

    def recv(self, *slots):
        for slot in slots:
            self.copy(slot, True).wait_recv()

    def stage_a(self):
        self.send(0, 2, 1, 3, 4, 5)

    def stage_b(self):
        self.recv(0)
        self.send(6)
        self.recv(2)
        self.send(7)
        self.recv(4)
        self.send(8, 9, 14)
        self.recv(1)
        self.send(12)
        self.recv(3)
        self.send(13)

    def stage_c(self):
        self.recv(6)
        self.send(10)
        self.recv(7)
        self.send(11, 15)

    def stage_d(self):
        self.recv(8)
        self.send(16)
        self.recv(9)
        self.send(17)
        self.recv(10, 11)
        self.send(18)

    def drain(self):
        every = self.buf.at[pl.ds(0, PEERS - 1)]
        remote(every, every, self.ss, self.rs.at[0], self.any_peer).wait_send()


class HiddenGather:
    def __init__(self, buf, ss, rs, feat):
        self.buf, self.ss, self.rs = buf, ss, rs
        z, xh = feat // 2, feat % 2
        self.rows = buf.shape[1] // 2

        def at(step, q):
            return ((z + 8 + step) % 8) * 2 + (xh if q == 0 else 1 - xh)

        up, down, partner = at(1, 0), at(-1, 0), at(0, 1)
        self.any_peer = {"feat": partner}
        self.table = {0: (at(0, 0), None, partner, partner)}
        for q in range(2):
            base = 1 + 8 * q
            for k in range(4):
                last = k == 3
                self.table[base + 2 * k] = (at(-k, q), 0 if last else None, up, at(-k - 1, q))
                self.table[base + 2 * k + 1] = (at(k, q), 1 if last else None, down, at(k + 1, q))

    def copy(self, slot, received):
        sent, half, target, incoming = self.table[slot]
        block = incoming if received else sent
        if half is None:
            ref = self.buf.at[block]
        else:
            ref = self.buf.at[block, pl.ds(half * self.rows, self.rows)]
        return remote(ref, ref, self.ss, self.rs.at[slot], {"feat": target})

    def send(self, *slots):
        for slot in slots:
            self.copy(slot, False).start()

    def recv(self, *slots):
        for slot in slots:
            self.copy(slot, True).wait_recv()

    def step(self, q, k):
        base = 1 + 8 * q + 2 * k
        if k:
            self.recv(base - 2, base - 1)
        self.send(base, base + 1)

    def drain(self):
        every = self.buf.at[pl.ds(0, PEERS - 1)]
        remote(every, every, self.ss, self.rs.at[0], self.any_peer).wait_send()


def exchange(axis, me, source, dst, ss, rs):
    others = dst.at[pl.ds(0, PEERS - 1)]

    def start():
        def step(j, carry):
            peer = (me + j) % PEERS
            remote(source(peer), dst.at[me], ss, rs, {axis: peer}).start()
            return carry

        lax.fori_loop(1, PEERS, step, 0)

    def all_of_them():
        return remote(others, others, ss, rs, {axis: (me + 1) % PEERS})

    return start, lambda: all_of_them().wait_recv(), lambda: all_of_them().wait_send()


def fold(values):
    return jnp.sum(values.reshape(CHUNK // 8, 8, COLS), axis=0)


def over_rows(blocks, step, init):
    per = ROWS // CHUNK

    def body(i, carry):
        return step(i // per, pl.ds(pl.multiple_of((i % per) * CHUNK, CHUNK), CHUNK), carry)

    return lax.fori_loop(0, blocks * per, body, init)


def local_statistics(ref):
    zero = jnp.zeros((8, COLS), F32)

    def add(block, rows, acc):
        return acc + fold(ref[rows].astype(F32))

    mean = jnp.sum(over_rows(1, add, zero), axis=0, keepdims=True) / ROWS

    def add_square(block, rows, acc):
        off = ref[rows].astype(F32) - mean
        return acc + fold(off * off)

    return mean, jnp.sum(over_rows(1, add_square, zero), axis=0, keepdims=True)


def merge_statistics(stats, view, batch):
    zero = jnp.zeros((1, COLS), F32)
    centre = lax.fori_loop(
        0, PEERS, lambda j, acc: acc + stats[view, j, 0:1], zero
    ) / PEERS

    def add(j, acc):
        off = stats[view, j, 0:1] - centre
        return acc + (stats[view, j, 1:2] + off * off * ROWS)

    spread = lax.fori_loop(0, PEERS, add, zero) / batch
    return centre, lax.rsqrt(spread + eps)


def kernel(
    packed, scale_ref,
    weight, loss_ref,
    one, two, grad, hid, normed_one, normed_two, fixed, raw, part, part_in, gram, spread, stats, sums, losses,
    local_sem, one_s, one_r, two_s, two_r, grad_s, grad_r, hid_s, hid_r,
    part_s, part_r, gram_s, gram_r, stats_s, stats_r, sums_s, sums_r, loss_s, loss_r,
):
    dp, feat = lax.axis_index("dp"), lax.axis_index("feat")
    batch = ROWS * PEERS
    width = COLS * PEERS

    local = [
        pltpu.make_async_copy(packed.at[0], two.at[dp], local_sem.at[0]),
        pltpu.make_async_copy(packed.at[1], one.at[dp], local_sem.at[1]),
        pltpu.make_async_copy(packed.at[2], raw, local_sem.at[2]),
    ]
    for copy in local:
        copy.start()

    barrier = pltpu.get_barrier_semaphore()

    def greet(j, carry):
        pl.semaphore_signal(
            barrier, inc=1, device_id={"dp": (dp + j) % PEERS}, device_id_type=MESH
        )
        pl.semaphore_signal(
            barrier, inc=1, device_id={"feat": (feat + j) % PEERS}, device_id_type=MESH
        )
        return carry

    lax.fori_loop(1, PEERS, greet, 0)
    for copy in local:
        copy.wait()

    gather_two = DpGather(two, two_s, two_r, dp)
    gather_one = DpGather(one, one_s, one_r, dp)
    gather_grad = DpGather(grad, grad_s, grad_r, dp)
    gather_hid = HiddenGather(hid, hid_s, hid_r, feat)
    stats_moves = [
        exchange("dp", dp, source(k), stats.at[k], stats_s.at[k], stats_r.at[k])
        for source, k in ((lambda k: lambda p: stats.at[k, dp], v) for v in range(2))
    ]
    part_moves, gram_moves = [
        [exchange("feat", feat, source(k), dst.at[k], ss.at[k], rs.at[k]) for k in range(2)]
        for source, dst, ss, rs in (
            (lambda k: lambda p: part.at[k, p], part_in, part_s, part_r),
            (lambda k: lambda p: gram.at[k, feat], gram, gram_s, gram_r),
        )
    ]
    pl.semaphore_wait(barrier, 2 * (PEERS - 1))

    gather_two.stage_a()

    def start_statistics(view, buf):
        mean, square = local_statistics(buf.at[dp])
        stats[view, dp, 0:1] = mean
        stats[view, dp, 1:2] = square
        stats_moves[view][0]()

    start_statistics(0, two)
    hid[feat] = raw[...].T
    gather_hid.send(0)
    gather_hid.step(0, 0)
    gather_two.stage_b()
    stats_moves[0][1]()
    centre, inverse = merge_statistics(stats, 0, batch)

    def gram_pair(group, place, pair):
        def norm(block, rows, carry):
            values = two[2 * pair + block, rows].astype(F32)
            normed_two[2 * pair + block, rows] = ((values - centre) * inverse).astype(BF)
            return carry

        over_rows(2, norm, 0)
        tile = lax.dot_general(
            normed_two[dp],
            normed_two[pl.ds(2 * pair, 2)].reshape(2 * ROWS, COLS),
            (((1,), (1,)), ((), ())),
            preferred_element_type=F32,
        ).astype(BF)
        first = 4 * place
        part[group, first : first + 2] = tile[:, :ROWS].reshape(2, HALF, ROWS)
        part[group, first + 2 : first + 4] = tile[:, ROWS:].reshape(2, HALF, ROWS)

    def add_parts(group):
        part_in[group, feat] = part[group, feat]
        part_moves[group][1]()

        def add(j, acc):
            return acc + part_in[group, j].astype(F32)

        gram[group, feat] = lax.fori_loop(0, PEERS, add, jnp.zeros((HALF, ROWS), F32)).astype(BF)
        gram_moves[group][0]()

    for place, (pair, slot) in enumerate(gather_two.near):
        gather_two.recv(slot)
        gram_pair(0, place, pair)
    part_moves[0][0]()
    gather_hid.recv(0)
    gather_hid.step(1, 0)
    gather_two.stage_c()
    gather_two.recv(15)
    gram_pair(1, 0, gather_two.later[0][0])
    gather_hid.step(0, 1)
    add_parts(0)
    gather_two.stage_d()
    gather_one.stage_a()
    start_statistics(1, one)
    for place, (pair, slot) in list(enumerate(gather_two.later))[1:]:
        gather_two.recv(slot)
        gram_pair(1, place, pair)
    part_moves[1][0]()
    gather_hid.step(1, 1)
    gather_one.stage_b()
    add_parts(1)
    gather_hid.step(0, 2)

    stats_moves[1][1]()
    centre_one, inverse_one = merge_statistics(stats, 1, batch)

    def norm_pair(pair, acc):
        def norm(block, rows, acc):
            values = one[2 * pair + block, rows].astype(F32)
            normed = ((values - centre_one) * inverse_one).astype(BF)
            normed_one[2 * pair + block, rows] = normed
            return acc + fold(
                normed.astype(F32) * normed_two[2 * pair + block, rows].astype(F32)
            )

        return over_rows(2, norm, acc)

    acc = jnp.zeros((8, COLS), F32)
    for pair, slot in gather_one.near:
        gather_one.recv(slot)
        acc = norm_pair(pair, acc)
    gather_one.stage_c()
    gather_hid.step(1, 2)
    gather_one.stage_d()
    for pair, slot in gather_one.later:
        gather_one.recv(slot)
        acc = norm_pair(pair, acc)
    corr = jnp.sum(acc, axis=0, keepdims=True) / batch
    scale = scale_ref[0] / batch
    weight_diag = scale * (-2.0 * (1.0 - corr) - 2.0 * off_weight * corr)

    def add_spread(group, pairs):
        for place, (pair, _) in enumerate(pairs):
            first = 4 * place
            rows = jnp.concatenate(
                [
                    gram[group, first : first + 2].reshape(ROWS, ROWS),
                    gram[group, first + 2 : first + 4].reshape(ROWS, ROWS),
                ],
                axis=1,
            )
            product = jnp.dot(
                rows,
                normed_one[pl.ds(2 * pair, 2)].reshape(2 * ROWS, COLS),
                preferred_element_type=F32,
            )
            if group == 0 and place == 0:
                spread[...] = product
            else:
                spread[...] += product

    gram_moves[0][1]()
    add_spread(0, gather_one.near)
    gram_moves[1][1]()
    add_spread(1, gather_one.later)
    factor = scale * (2.0 * off_weight / batch)
    zero = jnp.zeros((8, COLS), F32)

    def norm_step(block, rows, accs):
        raw_spread = spread[rows]
        share = normed_one[dp, rows].astype(F32)
        value = raw_spread * factor + normed_two[dp, rows].astype(F32) * weight_diag
        spread[rows] = value
        return (
            accs[0] + fold(value),
            accs[1] + fold(value * share),
            accs[2] + fold(raw_spread * share),
        )

    accs = over_rows(1, norm_step, (zero, zero, zero))
    sum_grad = jnp.sum(accs[0], axis=0, keepdims=True)
    sum_cross = jnp.sum(accs[1], axis=0, keepdims=True)
    near_grad = sum_grad / ROWS
    near_cross = sum_cross / ROWS

    def grad_step(block, rows, carry):
        share = normed_one[dp, rows].astype(F32)
        grad[dp, rows] = (spread[rows] - near_grad - share * near_cross).astype(BF)
        return carry

    over_rows(1, grad_step, 0)
    gather_grad.stage_a()
    square = jnp.sum(accs[2], axis=0, keepdims=True) / (float(batch) * float(batch))
    terms = off_weight * square + (
        (1.0 - corr) * (1.0 - corr) - off_weight * corr * corr
    ) * (1.0 / PEERS)
    lanes = terms[:, :128]
    for k in range(1, COLS // 128):
        lanes = lanes + terms[:, k * 128 : (k + 1) * 128]
    sums[dp, 0:1, :COLS] = sum_grad
    sums[dp, 1:2, :COLS] = sum_cross
    sums[dp, 0:1, COLS:] = lanes
    sums[dp, 1:2, COLS:] = jnp.zeros_like(lanes)
    sums_start, sums_recv, sums_send = exchange(
        "dp", dp, lambda p: sums.at[dp], sums, sums_s, sums_r
    )
    sums_start()
    gather_hid.step(0, 3)
    gather_grad.stage_b()
    sums_recv()
    total = lax.fori_loop(
        0, PEERS, lambda j, acc: acc + sums[j], jnp.zeros((2, COLS + 128), F32)
    )
    losses[feat] = total[:, COLS:]
    loss_start, loss_recv, loss_send = exchange(
        "feat", feat, lambda p: losses.at[feat], losses, loss_s, loss_r
    )
    loss_start()
    gather_hid.step(1, 3)
    mean_grad = total[0:1, :COLS] / batch
    mean_cross = total[1:2, :COLS] / batch

    def fix_pair(pair, place):
        for block in range(2):
            at = 2 * pair + block
            shift = mean_grad - sums[at, 0:1, :COLS] / ROWS
            tilt = mean_cross - sums[at, 1:2, :COLS] / ROWS

            def fix(i, rows, carry):
                share = normed_one[at, rows].astype(F32)
                value = grad[at, rows].astype(F32) - shift - share * tilt
                fixed[2 * place + block, rows] = (value * inverse_one).astype(BF)
                return carry

            over_rows(1, fix, 0)

    def add_pairs(pairs, first):
        count = 2 * len(pairs)

        def step(i, carry):
            rows = pl.ds(pl.multiple_of(i * 512, 512), 512)
            lhs = jnp.concatenate(
                [hid[2 * pair + block, rows] for pair in pairs for block in range(2)], axis=1
            )
            product = jnp.dot(
                lhs, fixed[:count].reshape(count * ROWS, COLS), preferred_element_type=F32
            )
            if first:
                weight[rows] = product
            else:
                weight[rows] += product
            return carry

        lax.fori_loop(0, COLS // 512, step, 0)

    def finish_pairs(group, first):
        for place, (pair, slot) in enumerate(group):
            gather_grad.recv(slot)
            fix_pair(pair, place)
        add_pairs([pair for pair, _ in group], first)

    gather_hid.recv(7, 8, 15, 16)
    finish_pairs(gather_grad.near[:2], True)
    gather_grad.stage_c()
    finish_pairs(gather_grad.near[2:], False)
    gather_grad.stage_d()
    finish_pairs(gather_grad.later[:1], False)
    finish_pairs(gather_grad.later[1:], False)

    loss_recv()
    all_loss = lax.fori_loop(
        0, PEERS, lambda j, acc: acc + losses[j], jnp.zeros((2, 128), F32)
    )
    loss_ref[0] = jnp.sum(all_loss) / width
    gather_two.drain()
    gather_one.drain()
    gather_grad.drain()
    gather_hid.drain()
    for group in range(2):
        stats_moves[group][2]()
        part_moves[group][2]()
        gram_moves[group][2]()
    sums_send()
    loss_send()


def body(z_one, z_two, hidden_in, grad_acc, loss_scale):
    in_hbm = pl.BlockSpec(memory_space=pltpu.HBM)
    in_smem = pl.BlockSpec(memory_space=pltpu.SMEM)
    dma = pltpu.SemaphoreType.DMA
    weight_grad, loss = pl.pallas_call(
        kernel,
        out_shape=(
            jax.ShapeDtypeStruct((COLS, COLS), F32),
            jax.ShapeDtypeStruct((1,), F32),
        ),
        in_specs=[in_hbm, in_smem],
        out_specs=(pl.BlockSpec(memory_space=pltpu.VMEM), in_smem),
        scratch_shapes=[
            pltpu.VMEM((PEERS, ROWS, COLS), BF),
            pltpu.VMEM((PEERS, ROWS, COLS), BF),
            pltpu.VMEM((PEERS, ROWS, COLS), BF),
            pltpu.VMEM((PEERS, COLS, ROWS), BF),
            pltpu.VMEM((PEERS, ROWS, COLS), BF),
            pltpu.VMEM((PEERS, ROWS, COLS), BF),
            pltpu.VMEM((6, ROWS, COLS), BF),
            pltpu.VMEM((ROWS, COLS), BF),
            pltpu.VMEM((2, PEERS, HALF, ROWS), BF),
            pltpu.VMEM((2, PEERS, HALF, ROWS), BF),
            pltpu.VMEM((2, PEERS, HALF, ROWS), BF),
            pltpu.VMEM((ROWS, COLS), F32),
            pltpu.VMEM((2, PEERS, 2, COLS), F32),
            pltpu.VMEM((PEERS, 2, COLS + 128), F32),
            pltpu.VMEM((PEERS, 2, 128), F32),
            dma((3,)),
        ]
        + [dma, dma((19,))] * 3
        + [dma, dma((17,))]
        + [dma((2,))] * 6
        + [dma] * 4,
        compiler_params=pltpu.CompilerParams(
            collective_id=0, has_side_effects=True, vmem_limit_bytes=48 << 20
        ),
        cost_estimate=pl.CostEstimate(
            flops=6 * 10**9, bytes_accessed=8 * 10**6, transcendentals=0
        ),
        name="barlow",
    )(jnp.stack([z_two, z_one, hidden_in]), loss_scale)
    return grad_acc + weight_grad, loss


def solution(mesh):
    placed = (P("dp", "feat"), P("dp", "feat"), P("feat", "dp"), P("dp", "feat"), P())
    return jax.shard_map(
        body, mesh=mesh, in_specs=placed, out_specs=(P("dp", "feat"), P()), check_vma=False
    )
```

```python
import jax
import jax.numpy as jnp
from jax import lax
from jax.experimental import pallas as pl
from jax.experimental.pallas import tpu as pltpu
from jax.sharding import PartitionSpec as P

MESH = pl.DeviceIdType.MESH
BF = jnp.bfloat16
F32 = jnp.float32
off_weight = 0.0051
eps = 1e-05
PEERS = 16
ROWS = 128
COLS = 1024
HALF = ROWS // 2
CHUNK = 64


def remote(src, dst, ss, rs, device):
    return pltpu.make_async_remote_copy(
        src_ref=src, dst_ref=dst, send_sem=ss, recv_sem=rs, device_id=device, device_id_type=MESH
    )


class DpGather:
    def __init__(self, buf, ss, rs, dp):
        self.buf, self.ss, self.rs = buf, ss, rs
        core, y, x = dp % 2, (dp // 2) % 4, dp // 8

        def block(x_, y_):
            return (x_ * 4 + y_) * 2 + core

        low, high, far = (y + 3) % 4, (y + 1) % 4, (y + 2) % 4
        self.own, self.ym, self.yp, self.y2 = (block(x, v) for v in (y, low, high, far))
        self.xo, self.xm, self.xp, self.x2 = (block(1 - x, v) for v in (y, low, high, far))
        self.flip = 1 - 2 * core
        self.any_peer = {"dp": self.xo}
        self.table = [
            (self.own, 0, self.yp, self.ym),
            (self.own, 1, self.yp, self.ym),
            (self.own, 1, self.ym, self.yp),
            (self.own, 0, self.ym, self.yp),
            (self.own, None, self.xo, self.xo),
            (self.own, None, None, self.own),
            (self.ym, 0, self.yp, self.y2),
            (self.yp, 1, self.ym, self.y2),
            (self.xo, None, self.yp, self.xm),
            (self.xo, None, self.ym, self.xp),
            (self.y2, 0, self.xo, self.x2),
            (self.y2, 1, self.xo, self.x2),
            (self.ym, None, None, self.ym),
            (self.yp, None, None, self.yp),
            (self.xo, None, None, self.xo),
            (self.y2, None, None, self.y2),
            (self.xm, None, None, self.xm),
            (self.xp, None, None, self.xp),
            (self.x2, None, None, self.x2),
        ]
        self.near = [(v // 2, slot) for v, slot in ((self.own, 5), (self.xo, 14), (self.ym, 12), (self.yp, 13))]
        self.later = [(v // 2, slot) for v, slot in ((self.y2, 15), (self.xm, 16), (self.xp, 17), (self.x2, 18))]

    def copy(self, slot, received):
        sent, half, target, incoming = self.table[slot]
        if target is None:
            target = self.own + self.flip
            incoming = incoming + self.flip
        block = incoming if received else sent
        ref = self.buf.at[block]
        if half is not None:
            ref = self.buf.at[block, pl.ds(half * HALF, HALF)]
        return remote(ref, ref, self.ss, self.rs.at[slot], {"dp": target})

    def send(self, *slots):
        for slot in slots:
            self.copy(slot, False).start()

    def recv(self, *slots):
        for slot in slots:
            self.copy(slot, True).wait_recv()

    def stage_a(self):
        self.send(0, 2, 1, 3, 4, 5)

    def stage_b(self):
        self.recv(0)
        self.send(6)
        self.recv(2)
        self.send(7)
        self.recv(4)
        self.send(8, 9, 14)
        self.recv(1)
        self.send(12)
        self.recv(3)
        self.send(13)

    def stage_c(self):
        self.recv(6)
        self.send(10)
        self.recv(7)
        self.send(11, 15)

    def stage_d(self):
        self.recv(8)
        self.send(16)
        self.recv(9)
        self.send(17)
        self.recv(10, 11)
        self.send(18)

    def drain(self):
        every = self.buf.at[pl.ds(0, PEERS - 1)]
        remote(every, every, self.ss, self.rs.at[0], self.any_peer).wait_send()


class HiddenGather:
    def __init__(self, buf, ss, rs, feat):
        self.buf, self.ss, self.rs = buf, ss, rs
        z, xh = feat // 2, feat % 2
        self.rows = buf.shape[1] // 2

        def at(step, q):
            return ((z + 8 + step) % 8) * 2 + (xh if q == 0 else 1 - xh)

        up, down, partner = at(1, 0), at(-1, 0), at(0, 1)
        self.any_peer = {"feat": partner}
        self.table = {0: (at(0, 0), None, partner, partner)}
        for q in range(2):
            base = 1 + 8 * q
            for k in range(4):
                last = k == 3
                self.table[base + 2 * k] = (at(-k, q), 0 if last else None, up, at(-k - 1, q))
                self.table[base + 2 * k + 1] = (at(k, q), 1 if last else None, down, at(k + 1, q))

    def copy(self, slot, received):
        sent, half, target, incoming = self.table[slot]
        block = incoming if received else sent
        if half is None:
            ref = self.buf.at[block]
        else:
            ref = self.buf.at[block, pl.ds(half * self.rows, self.rows)]
        return remote(ref, ref, self.ss, self.rs.at[slot], {"feat": target})

    def send(self, *slots):
        for slot in slots:
            self.copy(slot, False).start()

    def recv(self, *slots):
        for slot in slots:
            self.copy(slot, True).wait_recv()

    def step(self, q, k):
        base = 1 + 8 * q + 2 * k
        if k:
            self.recv(base - 2, base - 1)
        self.send(base, base + 1)

    def drain(self):
        every = self.buf.at[pl.ds(0, PEERS - 1)]
        remote(every, every, self.ss, self.rs.at[0], self.any_peer).wait_send()


def exchange(axis, me, source, dst, ss, rs):
    others = dst.at[pl.ds(0, PEERS - 1)]

    def start():
        def step(j, carry):
            peer = (me + j) % PEERS
            remote(source(peer), dst.at[me], ss, rs, {axis: peer}).start()
            return carry

        lax.fori_loop(1, PEERS, step, 0)

    def all_of_them():
        return remote(others, others, ss, rs, {axis: (me + 1) % PEERS})

    return start, lambda: all_of_them().wait_recv(), lambda: all_of_them().wait_send()


def fold(values):
    return jnp.sum(values.reshape(CHUNK // 8, 8, COLS), axis=0)


def over_rows(blocks, step, init):
    per = ROWS // CHUNK

    def body(i, carry):
        return step(i // per, pl.ds(pl.multiple_of((i % per) * CHUNK, CHUNK), CHUNK), carry)

    return lax.fori_loop(0, blocks * per, body, init)


def local_statistics(ref):
    zero = jnp.zeros((8, COLS), F32)

    def add(block, rows, acc):
        return acc + fold(ref[rows].astype(F32))

    mean = jnp.sum(over_rows(1, add, zero), axis=0, keepdims=True) / ROWS

    def add_square(block, rows, acc):
        off = ref[rows].astype(F32) - mean
        return acc + fold(off * off)

    return mean, jnp.sum(over_rows(1, add_square, zero), axis=0, keepdims=True)


def merge_statistics(stats, view, batch):
    zero = jnp.zeros((1, COLS), F32)
    centre = lax.fori_loop(
        0, PEERS, lambda j, acc: acc + stats[view, j, 0:1], zero
    ) / PEERS

    def add(j, acc):
        off = stats[view, j, 0:1] - centre
        return acc + (stats[view, j, 1:2] + off * off * ROWS)

    spread = lax.fori_loop(0, PEERS, add, zero) / batch
    return centre, lax.rsqrt(spread + eps)


def kernel(
    packed, scale_ref,
    weight, loss_ref,
    one, two, grad, hid, normed_one, normed_two, fixed, raw, part, part_in, gram, spread, stats, sums, losses, length,
    local_sem, one_s, one_r, two_s, two_r, grad_s, grad_r, hid_s, hid_r,
    part_s, part_r, gram_s, gram_r, stats_s, stats_r, sums_s, sums_r, loss_s, loss_r,
):
    dp, feat = lax.axis_index("dp"), lax.axis_index("feat")
    batch = ROWS * PEERS
    width = COLS * PEERS

    local = [
        pltpu.make_async_copy(packed.at[0], two.at[dp], local_sem.at[0]),
        pltpu.make_async_copy(packed.at[1], one.at[dp], local_sem.at[1]),
        pltpu.make_async_copy(packed.at[2], raw, local_sem.at[2]),
    ]
    for copy in local:
        copy.start()

    barrier = pltpu.get_barrier_semaphore()

    def greet(j, carry):
        pl.semaphore_signal(
            barrier, inc=1, device_id={"dp": (dp + j) % PEERS}, device_id_type=MESH
        )
        pl.semaphore_signal(
            barrier, inc=1, device_id={"feat": (feat + j) % PEERS}, device_id_type=MESH
        )
        return carry

    lax.fori_loop(1, PEERS, greet, 0)
    for copy in local:
        copy.wait()

    gather_two = DpGather(two, two_s, two_r, dp)
    gather_one = DpGather(one, one_s, one_r, dp)
    gather_grad = DpGather(grad, grad_s, grad_r, dp)
    gather_hid = HiddenGather(hid, hid_s, hid_r, feat)
    stats_moves = [
        exchange("dp", dp, source(k), stats.at[k], stats_s.at[k], stats_r.at[k])
        for source, k in ((lambda k: lambda p: stats.at[k, dp], v) for v in range(2))
    ]
    part_moves, gram_moves = [
        [exchange("feat", feat, source(k), dst.at[k], ss.at[k], rs.at[k]) for k in range(2)]
        for source, dst, ss, rs in (
            (lambda k: lambda p: part.at[k, p], part_in, part_s, part_r),
            (lambda k: lambda p: gram.at[k, feat], gram, gram_s, gram_r),
        )
    ]
    pl.semaphore_wait(barrier, 2 * (PEERS - 1))

    gather_two.stage_a()

    def start_statistics(view, buf):
        mean, square = local_statistics(buf.at[dp])
        stats[view, dp, 0:1] = mean
        stats[view, dp, 1:2] = square
        stats_moves[view][0]()

    start_statistics(0, two)
    hid[feat] = raw[...].T
    gather_hid.send(0)
    gather_hid.step(0, 0)
    gather_two.stage_b()
    gather_hid.step(0, 1)
    stats_moves[0][1]()
    centre, inverse = merge_statistics(stats, 0, batch)

    def gram_pair(group, place, pair):
        def norm(block, rows, carry):
            values = two[2 * pair + block, rows].astype(F32)
            normed_two[2 * pair + block, rows] = ((values - centre) * inverse).astype(BF)
            return carry

        over_rows(2, norm, 0)
        tile = lax.dot_general(
            normed_two[dp],
            normed_two[pl.ds(2 * pair, 2)].reshape(2 * ROWS, COLS),
            (((1,), (1,)), ((), ())),
            preferred_element_type=F32,
        ).astype(BF)
        first = 4 * place
        part[group, first : first + 2] = tile[:, :ROWS].reshape(2, HALF, ROWS)
        part[group, first + 2 : first + 4] = tile[:, ROWS:].reshape(2, HALF, ROWS)

    def add_parts(group):
        part_in[group, feat] = part[group, feat]
        part_moves[group][1]()

        def add(j, acc):
            return acc + part_in[group, j].astype(F32)

        gram[group, feat] = lax.fori_loop(0, PEERS, add, jnp.zeros((HALF, ROWS), F32)).astype(BF)
        gram_moves[group][0]()

    def gram_pairs(group, first, pairs):
        for place, (pair, slot) in enumerate(pairs):
            gather_two.recv(slot)
            gram_pair(group, first + place, pair)

    gram_pairs(0, 0, gather_two.near[:2])
    gather_two.stage_c()
    gather_hid.recv(0)
    gather_hid.step(1, 0)
    gram_pairs(0, 2, gather_two.near[2:])
    part_moves[0][0]()
    gram_pairs(1, 0, gather_two.later[:1])
    gather_two.stage_d()
    gather_one.stage_a()
    gram_pairs(1, 1, gather_two.later[1:])
    part_moves[1][0]()
    start_statistics(1, one)
    add_parts(0)
    gather_one.stage_b()
    stats_moves[1][1]()
    centre_one, inverse_one = merge_statistics(stats, 1, batch)

    def norm_pair(pair, acc):
        for block in range(2):
            at = 2 * pair + block

            def norm(i, rows, accs):
                values = one[at, rows].astype(F32)
                normed = ((values - centre_one) * inverse_one).astype(BF)
                normed_one[at, rows] = normed
                share = normed.astype(F32)
                return (
                    accs[0] + fold(share * normed_two[at, rows].astype(F32)),
                    accs[1] + fold(share * share),
                )

            acc, norms = over_rows(1, norm, (acc, jnp.zeros((8, COLS), F32)))
            norms = jnp.sum(norms, axis=0, keepdims=True)
            length[at] = 1.0 / jnp.maximum(norms, 1e-3)
        return acc

    acc = jnp.zeros((8, COLS), F32)
    gather_one.stage_c()
    for pair, slot in gather_one.near:
        gather_one.recv(slot)
        acc = norm_pair(pair, acc)
    add_parts(1)
    gather_hid.step(0, 2)
    gather_one.stage_d()
    for pair, slot in gather_one.later:
        gather_one.recv(slot)
        acc = norm_pair(pair, acc)
    corr = jnp.sum(acc, axis=0, keepdims=True) / batch
    scale = scale_ref[0] / batch
    weight_diag = scale * (-2.0 * (1.0 - corr) - 2.0 * off_weight * corr)

    def add_spread(group, pairs):
        for place, (pair, _) in enumerate(pairs):
            first = 4 * place
            rows = jnp.concatenate(
                [
                    gram[group, first : first + 2].reshape(ROWS, ROWS),
                    gram[group, first + 2 : first + 4].reshape(ROWS, ROWS),
                ],
                axis=1,
            )
            product = jnp.dot(
                rows,
                normed_one[pl.ds(2 * pair, 2)].reshape(2 * ROWS, COLS),
                preferred_element_type=F32,
            )
            if group == 0 and place == 0:
                spread[...] = product
            else:
                spread[...] += product

    gram_moves[0][1]()
    add_spread(0, gather_one.near)
    gather_hid.step(1, 1)
    gram_moves[1][1]()
    add_spread(1, gather_one.later)
    factor = scale * (2.0 * off_weight / batch)
    zero = jnp.zeros((8, COLS), F32)

    def norm_step(block, rows, accs):
        raw_spread = spread[rows]
        share = normed_one[dp, rows].astype(F32)
        value = raw_spread * factor + normed_two[dp, rows].astype(F32) * weight_diag
        spread[rows] = value
        return (
            accs[0] + fold(value),
            accs[1] + fold(value * share),
            accs[2] + fold(raw_spread * share),
        )

    accs = over_rows(1, norm_step, (zero, zero, zero))
    sum_grad = jnp.sum(accs[0], axis=0, keepdims=True)
    sum_cross = jnp.sum(accs[1], axis=0, keepdims=True)
    near_tilt = sum_cross * length[dp]

    def grad_step(block, rows, carry):
        share = normed_one[dp, rows].astype(F32)
        grad[dp, rows] = (spread[rows] - share * near_tilt).astype(BF)
        return carry

    over_rows(1, grad_step, 0)
    gather_grad.stage_a()
    gather_hid.step(0, 3)
    square = jnp.sum(accs[2], axis=0, keepdims=True) / (float(batch) * float(batch))
    terms = off_weight * square + (
        (1.0 - corr) * (1.0 - corr) - off_weight * corr * corr
    ) * (1.0 / PEERS)
    lanes = terms[:, :128]
    for k in range(1, COLS // 128):
        lanes = lanes + terms[:, k * 128 : (k + 1) * 128]
    sums[dp, 0:1, :COLS] = sum_grad
    sums[dp, 1:2, :COLS] = sum_cross
    sums[dp, 0:1, COLS:] = lanes
    sums[dp, 1:2, COLS:] = jnp.zeros_like(lanes)
    sums_start, sums_recv, sums_send = exchange(
        "dp", dp, lambda p: sums.at[dp], sums, sums_s, sums_r
    )
    sums_start()
    gather_grad.stage_b()
    gather_hid.step(1, 2)
    gather_grad.stage_c()
    gather_hid.step(1, 3)
    sums_recv()
    total = lax.fori_loop(
        0, PEERS, lambda j, acc: acc + sums[j], jnp.zeros((2, COLS + 128), F32)
    )
    losses[feat] = total[:, COLS:]
    loss_start, loss_recv, loss_send = exchange(
        "feat", feat, lambda p: losses.at[feat], losses, loss_s, loss_r
    )
    loss_start()
    mean_grad = total[0:1, :COLS] / batch
    mean_cross = total[1:2, :COLS] / batch

    def fix_pair(pair, place):
        for block in range(2):
            at = 2 * pair + block
            tilt = mean_cross - sums[at, 1:2, :COLS] * length[at]

            def fix(i, rows, carry):
                share = normed_one[at, rows].astype(F32)
                value = grad[at, rows].astype(F32) - mean_grad - share * tilt
                fixed[2 * place + block, rows] = (value * inverse_one).astype(BF)
                return carry

            over_rows(1, fix, 0)

    def add_pairs(pairs, first):
        count = 2 * len(pairs)

        def step(i, carry):
            rows = pl.ds(pl.multiple_of(i * 1024, 1024), 1024)
            lhs = jnp.concatenate(
                [hid[2 * pair + block, rows] for pair in pairs for block in range(2)], axis=1
            )
            product = jnp.dot(
                lhs, fixed[:count].reshape(count * ROWS, COLS), preferred_element_type=F32
            )
            if first:
                weight[rows] = product
            else:
                weight[rows] += product
            return carry

        lax.fori_loop(0, COLS // 1024, step, 0)

    def finish_pairs(group, first):
        for place, (pair, slot) in enumerate(group):
            gather_grad.recv(slot)
            fix_pair(pair, place)
        add_pairs([pair for pair, _ in group], first)

    gather_hid.recv(7, 8, 15, 16)
    finish_pairs(gather_grad.near[:2], True)
    finish_pairs(gather_grad.near[2:], False)
    finish_pairs(gather_grad.later[:1], False)
    gather_grad.stage_d()
    finish_pairs(gather_grad.later[1:], False)

    loss_recv()
    all_loss = lax.fori_loop(
        0, PEERS, lambda j, acc: acc + losses[j], jnp.zeros((2, 128), F32)
    )
    loss_ref[0] = jnp.sum(all_loss) / width
    gather_two.drain()
    gather_one.drain()
    gather_grad.drain()
    gather_hid.drain()
    for group in range(2):
        stats_moves[group][2]()
        part_moves[group][2]()
        gram_moves[group][2]()
    sums_send()
    loss_send()


def body(z_one, z_two, hidden_in, grad_acc, loss_scale):
    in_hbm = pl.BlockSpec(memory_space=pltpu.HBM)
    in_smem = pl.BlockSpec(memory_space=pltpu.SMEM)
    dma = pltpu.SemaphoreType.DMA
    weight_grad, loss = pl.pallas_call(
        kernel,
        out_shape=(
            jax.ShapeDtypeStruct((COLS, COLS), F32),
            jax.ShapeDtypeStruct((1,), F32),
        ),
        in_specs=[in_hbm, in_smem],
        out_specs=(pl.BlockSpec(memory_space=pltpu.VMEM), in_smem),
        scratch_shapes=[
            pltpu.VMEM((PEERS, ROWS, COLS), BF),
            pltpu.VMEM((PEERS, ROWS, COLS), BF),
            pltpu.VMEM((PEERS, ROWS, COLS), BF),
            pltpu.VMEM((PEERS, COLS, ROWS), BF),
            pltpu.VMEM((PEERS, ROWS, COLS), BF),
            pltpu.VMEM((PEERS, ROWS, COLS), BF),
            pltpu.VMEM((6, ROWS, COLS), BF),
            pltpu.VMEM((ROWS, COLS), BF),
            pltpu.VMEM((2, PEERS, HALF, ROWS), BF),
            pltpu.VMEM((2, PEERS, HALF, ROWS), BF),
            pltpu.VMEM((2, PEERS, HALF, ROWS), BF),
            pltpu.VMEM((ROWS, COLS), F32),
            pltpu.VMEM((2, PEERS, 2, COLS), F32),
            pltpu.VMEM((PEERS, 2, COLS + 128), F32),
            pltpu.VMEM((PEERS, 2, 128), F32),
            pltpu.VMEM((PEERS, 1, COLS), F32),
            dma((3,)),
        ]
        + [dma, dma((19,))] * 3
        + [dma, dma((17,))]
        + [dma((2,))] * 6
        + [dma] * 4,
        compiler_params=pltpu.CompilerParams(
            collective_id=0, has_side_effects=True, vmem_limit_bytes=48 << 20
        ),
        cost_estimate=pl.CostEstimate(
            flops=6 * 10**9, bytes_accessed=8 * 10**6, transcendentals=0
        ),
        name="barlow",
    )(jnp.stack([z_two, z_one, hidden_in]), loss_scale)
    return grad_acc + weight_grad, loss


def solution(mesh):
    placed = (P("dp", "feat"), P("dp", "feat"), P("feat", "dp"), P("dp", "feat"), P())
    return jax.shard_map(
        body, mesh=mesh, in_specs=placed, out_specs=(P("dp", "feat"), P()), check_vma=False
    )
```

```python
import jax
import jax.numpy as jnp
from jax import lax
from jax.experimental import pallas as pl
from jax.experimental.pallas import tpu as pltpu
from jax.sharding import PartitionSpec as P

MESH = pl.DeviceIdType.MESH
BF = jnp.bfloat16
F32 = jnp.float32
off_weight = 0.0051
eps = 1e-05
PEERS = 16
ROWS = 128
COLS = 1024
HALF = ROWS // 2
PIECE = (48, 32)
CHUNK = 64


def remote(src, dst, ss, rs, device):
    return pltpu.make_async_remote_copy(
        src_ref=src, dst_ref=dst, send_sem=ss, recv_sem=rs, device_id=device, device_id_type=MESH
    )


class DpGather:
    def __init__(self, buf, ss, rs, dp):
        self.buf, self.ss, self.rs = buf, ss, rs
        core, y, x = dp % 2, (dp // 2) % 4, dp // 8

        def block(x_, y_):
            return (x_ * 4 + y_) * 2 + core

        low, high, far = (y + 3) % 4, (y + 1) % 4, (y + 2) % 4
        self.own, self.ym, self.yp, self.y2 = (block(x, v) for v in (y, low, high, far))
        self.xo, self.xm, self.xp, self.x2 = (block(1 - x, v) for v in (y, low, high, far))
        self.flip = 1 - 2 * core
        self.any_peer = {"dp": self.xo}
        self.table = [
            (self.own, 0, self.yp, self.ym),
            (self.own, 1, self.yp, self.ym),
            (self.own, 1, self.ym, self.yp),
            (self.own, 0, self.ym, self.yp),
            (self.own, None, self.xo, self.xo),
            (self.own, None, None, self.own),
            (self.ym, 0, self.yp, self.y2),
            (self.yp, 1, self.ym, self.y2),
            (self.xo, None, self.yp, self.xm),
            (self.xo, None, self.ym, self.xp),
            (self.y2, 0, self.xo, self.x2),
            (self.y2, 1, self.xo, self.x2),
            (self.ym, None, None, self.ym),
            (self.yp, None, None, self.yp),
            (self.xo, None, None, self.xo),
            (self.y2, None, None, self.y2),
            (self.xm, None, None, self.xm),
            (self.xp, None, None, self.xp),
            (self.x2, None, None, self.x2),
        ]
        self.near = [(v // 2, slot) for v, slot in ((self.own, 5), (self.xo, 14), (self.ym, 12), (self.yp, 13))]
        self.later = [(v // 2, slot) for v, slot in ((self.y2, 15), (self.xm, 16), (self.xp, 17), (self.x2, 18))]

    def copy(self, slot, received):
        sent, half, target, incoming = self.table[slot]
        if target is None:
            target = self.own + self.flip
            incoming = incoming + self.flip
        block = incoming if received else sent
        ref = self.buf.at[block]
        if half is not None:
            ref = self.buf.at[block, pl.ds(half * HALF, HALF)]
        return remote(ref, ref, self.ss, self.rs.at[slot], {"dp": target})

    def send(self, *slots):
        for slot in slots:
            self.copy(slot, False).start()

    def recv(self, *slots):
        for slot in slots:
            self.copy(slot, True).wait_recv()

    def stage_a(self):
        self.send(0, 2, 1, 3, 4, 5)

    def stage_b(self):
        self.recv(0)
        self.send(6)
        self.recv(2)
        self.send(7)
        self.recv(4)
        self.send(8, 9, 14)
        self.recv(1)
        self.send(12)
        self.recv(3)
        self.send(13)

    def stage_c(self):
        self.recv(6)
        self.send(10)
        self.recv(7)
        self.send(11, 15)

    def stage_d(self):
        self.recv(8)
        self.send(16)
        self.recv(9)
        self.send(17)
        self.recv(10, 11)
        self.send(18)

    def drain(self):
        every = self.buf.at[pl.ds(0, PEERS - 1)]
        remote(every, every, self.ss, self.rs.at[0], self.any_peer).wait_send()


class HiddenGather:
    def __init__(self, buf, ss, rs, feat):
        self.buf, self.ss, self.rs = buf, ss, rs
        z, xh = feat // 2, feat % 2
        self.rows = buf.shape[1] // 2

        def at(step, q):
            return ((z + 8 + step) % 8) * 2 + (xh if q == 0 else 1 - xh)

        up, down, partner = at(1, 0), at(-1, 0), at(0, 1)
        self.any_peer = {"feat": partner}
        self.table = {0: (at(0, 0), None, partner, partner)}
        for q in range(2):
            base = 1 + 8 * q
            for k in range(4):
                last = k == 3
                self.table[base + 2 * k] = (at(-k, q), 0 if last else None, up, at(-k - 1, q))
                self.table[base + 2 * k + 1] = (at(k, q), 1 if last else None, down, at(k + 1, q))

    def copy(self, slot, received):
        sent, half, target, incoming = self.table[slot]
        block = incoming if received else sent
        if half is None:
            ref = self.buf.at[block]
        else:
            ref = self.buf.at[block, pl.ds(half * self.rows, self.rows)]
        return remote(ref, ref, self.ss, self.rs.at[slot], {"feat": target})

    def send(self, *slots):
        for slot in slots:
            self.copy(slot, False).start()

    def recv(self, *slots):
        for slot in slots:
            self.copy(slot, True).wait_recv()

    def step(self, q, k):
        base = 1 + 8 * q + 2 * k
        if k:
            self.recv(base - 2, base - 1)
        self.send(base, base + 1)

    def drain(self):
        every = self.buf.at[pl.ds(0, PEERS - 1)]
        remote(every, every, self.ss, self.rs.at[0], self.any_peer).wait_send()


def exchange(axis, me, source, target, every, ss, rs):
    def start():
        def step(j, carry):
            peer = (me + j) % PEERS
            remote(source(peer), target, ss, rs, {axis: peer}).start()
            return carry

        lax.fori_loop(1, PEERS, step, 0)

    def all_of_them():
        return remote(every, every, ss, rs, {axis: (me + 1) % PEERS})

    return start, lambda: all_of_them().wait_recv(), lambda: all_of_them().wait_send()


def fold(values):
    return jnp.sum(values.reshape(CHUNK // 8, 8, COLS), axis=0)


def over_rows(blocks, step, init):
    per = ROWS // CHUNK

    def body(i, carry):
        return step(i // per, pl.ds(pl.multiple_of((i % per) * CHUNK, CHUNK), CHUNK), carry)

    return lax.fori_loop(0, blocks * per, body, init)


def local_statistics(ref):
    zero = jnp.zeros((8, COLS), F32)

    def add(block, rows, acc):
        return acc + fold(ref[rows].astype(F32))

    mean = jnp.sum(over_rows(1, add, zero), axis=0, keepdims=True) / ROWS

    def add_square(block, rows, acc):
        off = ref[rows].astype(F32) - mean
        return acc + fold(off * off)

    return mean, jnp.sum(over_rows(1, add_square, zero), axis=0, keepdims=True)


def merge_statistics(stats, view, batch):
    zero = jnp.zeros((1, COLS), F32)
    centre = lax.fori_loop(
        0, PEERS, lambda j, acc: acc + stats[view, j, 0:1], zero
    ) / PEERS

    def add(j, acc):
        off = stats[view, j, 0:1] - centre
        return acc + (stats[view, j, 1:2] + off * off * ROWS)

    spread = lax.fori_loop(0, PEERS, add, zero) / batch
    return centre, lax.rsqrt(spread + eps)


def kernel(
    packed, scale_ref,
    weight, loss_ref,
    one, two, grad, hid, normed_one, normed_two, fixed, raw, part, part_in, gram, spread, stats, sums, losses, length, mirror,
    local_sem, one_s, one_r, two_s, two_r, grad_s, grad_r, hid_s, hid_r,
    part_s, part_r, gram_s, gram_r, stats_s, stats_r, sums_s, sums_r, loss_s, loss_r, mirror_s, mirror_r,
):
    dp, feat = lax.axis_index("dp"), lax.axis_index("feat")
    batch = ROWS * PEERS
    width = COLS * PEERS

    local = [
        pltpu.make_async_copy(packed.at[0], two.at[dp], local_sem.at[0]),
        pltpu.make_async_copy(packed.at[1], one.at[dp], local_sem.at[1]),
        pltpu.make_async_copy(packed.at[2], raw, local_sem.at[2]),
    ]
    for copy in local:
        copy.start()

    barrier = pltpu.get_barrier_semaphore()

    def greet(j, carry):
        pl.semaphore_signal(
            barrier, inc=1, device_id={"dp": (dp + j) % PEERS}, device_id_type=MESH
        )
        pl.semaphore_signal(
            barrier, inc=1, device_id={"feat": (feat + j) % PEERS}, device_id_type=MESH
        )
        return carry

    lax.fori_loop(1, PEERS, greet, 0)
    for copy in local:
        copy.wait()

    gather_two = DpGather(two, two_s, two_r, dp)
    gather_one = DpGather(one, one_s, one_r, dp)
    gather_grad = DpGather(grad, grad_s, grad_r, dp)
    gather_hid = HiddenGather(hid, hid_s, hid_r, feat)
    stats_moves = [
        exchange(
            "dp", dp, lambda p, k=k: stats.at[k, dp], stats.at[k, dp],
            stats.at[k, pl.ds(0, PEERS - 1)], stats_s.at[k], stats_r.at[k],
        )
        for k in range(2)
    ]
    def piece(k, owner):
        return pl.ds(pl.multiple_of(owner * PIECE[k], 16), PIECE[k])

    part_moves = [
        exchange(
            "feat", feat, lambda p, k=k: part.at[k, piece(k, p)],
            part_in.at[k, feat, pl.ds(0, PIECE[k])],
            part_in.at[k, pl.ds(0, PEERS - 1), pl.ds(0, PIECE[k])], part_s.at[k], part_r.at[k],
        )
        for k in range(2)
    ]
    gram_moves = [
        exchange(
            "feat", feat, lambda p, k=k: gram.at[k, piece(k, feat)], gram.at[k, piece(k, feat)],
            gram.at[k, pl.ds(0, (PEERS - 1) * PIECE[k])], gram_s.at[k], gram_r.at[k],
        )
        for k in range(2)
    ]
    pl.semaphore_wait(barrier, 2 * (PEERS - 1))

    gather_two.stage_a()

    def start_statistics(view, buf):
        mean, square = local_statistics(buf.at[dp])
        stats[view, dp, 0:1] = mean
        stats[view, dp, 1:2] = square
        stats_moves[view][0]()

    start_statistics(0, two)
    hid[feat] = raw[...].T
    gather_hid.send(0)
    gather_hid.step(0, 0)
    gather_two.stage_b()
    gather_hid.step(0, 1)
    stats_moves[0][1]()
    centre, inverse = merge_statistics(stats, 0, batch)

    def norm_two(pair):
        def norm(block, rows, carry):
            values = two[2 * pair + block, rows].astype(F32)
            normed_two[2 * pair + block, rows] = ((values - centre) * inverse).astype(BF)
            return carry

        over_rows(2, norm, 0)

    def gram_tiles(group, place, first, count):
        tile = lax.dot_general(
            normed_two[dp],
            normed_two[pl.ds(first, count)].reshape(count * ROWS, COLS),
            (((1,), (1,)), ((), ())),
            preferred_element_type=F32,
        ).astype(BF)
        for k in range(count):
            rows = pl.ds((place + k) * ROWS, ROWS)
            part[group, rows] = tile[:, k * ROWS : (k + 1) * ROWS]

    def add_parts(group):
        size = PIECE[group]
        part_in[group, feat, :size] = part[group, piece(group, feat)]
        part_moves[group][1]()

        def add(j, acc):
            return acc + part_in[group, j, :size].astype(F32)

        total = lax.fori_loop(0, PEERS, add, jnp.zeros((size, ROWS), F32))
        gram[group, piece(group, feat)] = total.astype(BF)
        gram_moves[group][0]()

    core, y, x = dp % 2, (dp // 2) % 4, dp // 8
    by_x = jnp.where(x == 0, core, 1 - core)
    by_y = jnp.where(y < 2, core, 1 - core)
    pair_of = {
        name: getattr(gather_two, name) // 2 for name in ("own", "xo", "ym", "yp", "y2", "xm", "xp", "x2")
    }
    xo_block, y2_block, x2_block = (
        2 * pair_of[name] + kept for name, kept in (("xo", by_x), ("y2", by_y), ("x2", by_x))
    )

    def mirror_copy(group, place, target, slot):
        return remote(
            gram.at[group, pl.ds(place * ROWS, ROWS)],
            mirror.at[group, slot],
            mirror_s.at[group],
            mirror_r.at[group],
            {"dp": target},
        )

    mirror_sends = (
        [(2, xo_block, 2), (3, 2 * pair_of["ym"], core), (4, 2 * pair_of["ym"] + 1, core)],
        [
            (0, y2_block, 2),
            (1, 2 * pair_of["xm"], core),
            (2, 2 * pair_of["xm"] + 1, core),
            (3, x2_block, 3),
        ],
    )

    def mirror_start(group):
        for place, target, slot in mirror_sends[group]:
            mirror_copy(group, place, target, slot).start()

    def mirror_all(group):
        every = mirror.at[group, pl.ds(0, len(mirror_sends[group]))]
        return remote(every, every, mirror_s.at[group], mirror_r.at[group], {"dp": xo_block})

    part[0, 5 * ROWS :] = jnp.zeros((ROWS, ROWS), BF)
    gather_two.recv(5)
    norm_two(pair_of["own"])
    gram_tiles(0, 0, 2 * pair_of["own"], 2)
    gather_two.recv(14)
    norm_two(pair_of["xo"])
    gram_tiles(0, 2, xo_block, 1)
    gather_two.recv(12)
    norm_two(pair_of["ym"])
    gram_tiles(0, 3, 2 * pair_of["ym"], 2)
    part_moves[0][0]()
    gather_two.stage_c()
    gather_hid.recv(0)
    gather_hid.step(1, 0)
    gather_two.recv(13)
    norm_two(pair_of["yp"])
    gather_two.recv(15)
    norm_two(pair_of["y2"])
    gram_tiles(1, 0, y2_block, 1)
    gather_two.stage_d()
    gather_one.stage_a()
    gather_two.recv(16)
    norm_two(pair_of["xm"])
    gram_tiles(1, 1, 2 * pair_of["xm"], 2)
    gather_two.recv(18)
    norm_two(pair_of["x2"])
    gram_tiles(1, 3, x2_block, 1)
    part_moves[1][0]()
    gather_two.recv(17)
    norm_two(pair_of["xp"])
    start_statistics(1, one)
    add_parts(0)
    gather_hid.step(0, 2)
    gather_one.stage_b()
    stats_moves[1][1]()
    centre_one, inverse_one = merge_statistics(stats, 1, batch)

    def norm_pair(pair, acc):
        for block in range(2):
            at = 2 * pair + block

            def norm(i, rows, accs):
                values = one[at, rows].astype(F32)
                normed = ((values - centre_one) * inverse_one).astype(BF)
                normed_one[at, rows] = normed
                share = normed.astype(F32)
                return (
                    accs[0] + fold(share * normed_two[at, rows].astype(F32)),
                    accs[1] + fold(share * share),
                )

            acc, norms = over_rows(1, norm, (acc, jnp.zeros((8, COLS), F32)))
            norms = jnp.sum(norms, axis=0, keepdims=True)
            length[at] = 1.0 / jnp.maximum(norms, 1e-3)
        return acc

    acc = jnp.zeros((8, COLS), F32)
    gather_one.stage_c()
    for pair, slot in gather_one.near:
        gather_one.recv(slot)
        acc = norm_pair(pair, acc)
    add_parts(1)
    gram_moves[0][1]()
    mirror_start(0)
    gather_hid.step(1, 1)
    gather_one.stage_d()
    gather_hid.step(0, 3)
    for pair, slot in gather_one.later:
        gather_one.recv(slot)
        acc = norm_pair(pair, acc)
    corr = jnp.sum(acc, axis=0, keepdims=True) / batch
    scale = scale_ref[0] / batch
    weight_diag = scale * (-2.0 * (1.0 - corr) - 2.0 * off_weight * corr)

    def add_spread(group, terms):
        for k in range(0, len(terms), 2):
            some = terms[k : k + 2]
            product = jnp.dot(
                jnp.concatenate([tile for tile, _ in some], axis=1),
                jnp.concatenate([normed_one[block] for _, block in some], axis=0),
                preferred_element_type=F32,
            )
            if group == 0 and k == 0:
                spread[...] = product
            else:
                spread[...] += product

    def kept_tile(group, place):
        return gram[group, place * ROWS : (place + 1) * ROWS]

    def mirrored_tile(group, slot):
        return mirror[group, slot].T

    gram_moves[1][1]()
    mirror_start(1)
    mirror_all(0).wait_recv()
    add_spread(
        0,
        [
            (kept_tile(0, 0), 2 * pair_of["own"]),
            (kept_tile(0, 1), 2 * pair_of["own"] + 1),
            (kept_tile(0, 2), xo_block),
            (mirrored_tile(0, 2), 4 * pair_of["xo"] + 1 - xo_block),
            (kept_tile(0, 3), 2 * pair_of["ym"]),
            (kept_tile(0, 4), 2 * pair_of["ym"] + 1),
            (mirrored_tile(0, 0), 2 * pair_of["yp"]),
            (mirrored_tile(0, 1), 2 * pair_of["yp"] + 1),
        ],
    )
    gather_hid.step(1, 2)
    mirror_all(1).wait_recv()
    add_spread(
        1,
        [
            (kept_tile(1, 0), y2_block),
            (mirrored_tile(1, 2), 4 * pair_of["y2"] + 1 - y2_block),
            (kept_tile(1, 1), 2 * pair_of["xm"]),
            (kept_tile(1, 2), 2 * pair_of["xm"] + 1),
            (mirrored_tile(1, 0), 2 * pair_of["xp"]),
            (mirrored_tile(1, 1), 2 * pair_of["xp"] + 1),
            (kept_tile(1, 3), x2_block),
            (mirrored_tile(1, 3), 4 * pair_of["x2"] + 1 - x2_block),
        ],
    )
    factor = scale * (2.0 * off_weight / batch)
    zero = jnp.zeros((8, COLS), F32)

    def norm_step(block, rows, accs):
        raw_spread = spread[rows]
        share = normed_one[dp, rows].astype(F32)
        value = raw_spread * factor + normed_two[dp, rows].astype(F32) * weight_diag
        spread[rows] = value
        return (
            accs[0] + fold(value),
            accs[1] + fold(value * share),
            accs[2] + fold(raw_spread * share),
        )

    accs = over_rows(1, norm_step, (zero, zero, zero))
    sum_grad = jnp.sum(accs[0], axis=0, keepdims=True)
    sum_cross = jnp.sum(accs[1], axis=0, keepdims=True)
    near_tilt = sum_cross * length[dp]

    def grad_step(block, rows, carry):
        share = normed_one[dp, rows].astype(F32)
        grad[dp, rows] = (spread[rows] - share * near_tilt).astype(BF)
        return carry

    over_rows(1, grad_step, 0)
    gather_grad.stage_a()
    gather_hid.step(1, 3)
    square = jnp.sum(accs[2], axis=0, keepdims=True) / (float(batch) * float(batch))
    terms = off_weight * square + (
        (1.0 - corr) * (1.0 - corr) - off_weight * corr * corr
    ) * (1.0 / PEERS)
    lanes = terms[:, :128]
    for k in range(1, COLS // 128):
        lanes = lanes + terms[:, k * 128 : (k + 1) * 128]
    sums[dp, 0:1, :COLS] = sum_grad
    sums[dp, 1:2, :COLS] = sum_cross
    sums[dp, 0:1, COLS:] = lanes
    sums[dp, 1:2, COLS:] = jnp.zeros_like(lanes)
    sums_start, sums_recv, sums_send = exchange(
        "dp", dp, lambda p: sums.at[dp], sums.at[dp], sums.at[pl.ds(0, PEERS - 1)], sums_s, sums_r
    )
    sums_start()
    gather_grad.stage_b()
    gather_grad.stage_c()
    sums_recv()
    total = lax.fori_loop(
        0, PEERS, lambda j, acc: acc + sums[j], jnp.zeros((2, COLS + 128), F32)
    )
    losses[feat] = total[:, COLS:]
    loss_start, loss_recv, loss_send = exchange(
        "feat", feat, lambda p: losses.at[feat], losses.at[feat],
        losses.at[pl.ds(0, PEERS - 1)], loss_s, loss_r,
    )
    loss_start()
    mean_grad = total[0:1, :COLS] / batch
    mean_cross = total[1:2, :COLS] / batch

    def fix_pair(pair, place):
        for block in range(2):
            at = 2 * pair + block
            tilt = mean_cross - sums[at, 1:2, :COLS] * length[at]

            def fix(i, rows, carry):
                share = normed_one[at, rows].astype(F32)
                value = grad[at, rows].astype(F32) - mean_grad - share * tilt
                fixed[2 * place + block, rows] = (value * inverse_one).astype(BF)
                return carry

            over_rows(1, fix, 0)

    def add_pairs(pairs, first):
        count = 2 * len(pairs)

        def step(i, carry):
            rows = pl.ds(pl.multiple_of(i * 1024, 1024), 1024)
            lhs = jnp.concatenate(
                [hid[2 * pair + block, rows] for pair in pairs for block in range(2)], axis=1
            )
            product = jnp.dot(
                lhs, fixed[:count].reshape(count * ROWS, COLS), preferred_element_type=F32
            )
            if first:
                weight[rows] = product
            else:
                weight[rows] += product
            return carry

        lax.fori_loop(0, COLS // 1024, step, 0)

    def finish_pairs(group, first):
        for place, (pair, slot) in enumerate(group):
            gather_grad.recv(slot)
            fix_pair(pair, place)
        add_pairs([pair for pair, _ in group], first)

    gather_hid.recv(7, 8, 15, 16)
    finish_pairs(gather_grad.near[:2], True)
    finish_pairs(gather_grad.near[2:], False)
    finish_pairs(gather_grad.later[:1], False)
    gather_grad.stage_d()
    finish_pairs(gather_grad.later[1:], False)

    loss_recv()
    all_loss = lax.fori_loop(
        0, PEERS, lambda j, acc: acc + losses[j], jnp.zeros((2, 128), F32)
    )
    loss_ref[0] = jnp.sum(all_loss) / width
    gather_two.drain()
    gather_one.drain()
    gather_grad.drain()
    gather_hid.drain()
    for group in range(2):
        stats_moves[group][2]()
        part_moves[group][2]()
        gram_moves[group][2]()
        mirror_all(group).wait_send()
    sums_send()
    loss_send()


def body(z_one, z_two, hidden_in, grad_acc, loss_scale):
    in_hbm = pl.BlockSpec(memory_space=pltpu.HBM)
    in_smem = pl.BlockSpec(memory_space=pltpu.SMEM)
    dma = pltpu.SemaphoreType.DMA
    weight_grad, loss = pl.pallas_call(
        kernel,
        out_shape=(
            jax.ShapeDtypeStruct((COLS, COLS), F32),
            jax.ShapeDtypeStruct((1,), F32),
        ),
        in_specs=[in_hbm, in_smem],
        out_specs=(pl.BlockSpec(memory_space=pltpu.VMEM), in_smem),
        scratch_shapes=[
            pltpu.VMEM((PEERS, ROWS, COLS), BF),
            pltpu.VMEM((PEERS, ROWS, COLS), BF),
            pltpu.VMEM((PEERS, ROWS, COLS), BF),
            pltpu.VMEM((PEERS, COLS, ROWS), BF),
            pltpu.VMEM((PEERS, ROWS, COLS), BF),
            pltpu.VMEM((PEERS, ROWS, COLS), BF),
            pltpu.VMEM((6, ROWS, COLS), BF),
            pltpu.VMEM((ROWS, COLS), BF),
            pltpu.VMEM((2, 6 * ROWS, ROWS), BF),
            pltpu.VMEM((2, PEERS, PIECE[0], ROWS), BF),
            pltpu.VMEM((2, 6 * ROWS, ROWS), BF),
            pltpu.VMEM((ROWS, COLS), F32),
            pltpu.VMEM((2, PEERS, 2, COLS), F32),
            pltpu.VMEM((PEERS, 2, COLS + 128), F32),
            pltpu.VMEM((PEERS, 2, 128), F32),
            pltpu.VMEM((PEERS, 1, COLS), F32),
            pltpu.VMEM((2, 4, ROWS, ROWS), BF),
            dma((3,)),
        ]
        + [dma, dma((19,))] * 3
        + [dma, dma((17,))]
        + [dma((2,))] * 6
        + [dma] * 4
        + [dma((2,))] * 2,
        compiler_params=pltpu.CompilerParams(
            collective_id=0, has_side_effects=True, vmem_limit_bytes=48 << 20
        ),
        cost_estimate=pl.CostEstimate(
            flops=6 * 10**9, bytes_accessed=8 * 10**6, transcendentals=0
        ),
        name="barlow",
    )(jnp.stack([z_two, z_one, hidden_in]), loss_scale)
    return grad_acc + weight_grad, loss


def solution(mesh):
    placed = (P("dp", "feat"), P("dp", "feat"), P("feat", "dp"), P("dp", "feat"), P())
    return jax.shard_map(
        body, mesh=mesh, in_specs=placed, out_specs=(P("dp", "feat"), P()), check_vma=False
    )
```

```python
import jax
import jax.numpy as jnp
from jax import lax
from jax.experimental import pallas as pl
from jax.experimental.pallas import tpu as pltpu
from jax.sharding import PartitionSpec as P

MESH = pl.DeviceIdType.MESH
BF = jnp.bfloat16
F32 = jnp.float32
off_weight = 0.0051
eps = 1e-05
PEERS = 16
ROWS = 128
COLS = 1024
HALF = ROWS // 2
PIECE = (48, 32)
CHUNK = 64


def remote(src, dst, ss, rs, device):
    return pltpu.make_async_remote_copy(
        src_ref=src, dst_ref=dst, send_sem=ss, recv_sem=rs, device_id=device, device_id_type=MESH
    )


class DpGather:
    def __init__(self, buf, ss, rs, dp):
        self.buf, self.ss, self.rs = buf, ss, rs
        core, y, x = dp % 2, (dp // 2) % 4, dp // 8

        def block(x_, y_):
            return (x_ * 4 + y_) * 2 + core

        low, high, far = (y + 3) % 4, (y + 1) % 4, (y + 2) % 4
        self.own, self.ym, self.yp, self.y2 = (block(x, v) for v in (y, low, high, far))
        self.xo, self.xm, self.xp, self.x2 = (block(1 - x, v) for v in (y, low, high, far))
        self.flip = 1 - 2 * core
        self.any_peer = {"dp": self.xo}
        self.table = [
            (self.own, 0, self.yp, self.ym),
            (self.own, 1, self.yp, self.ym),
            (self.own, 1, self.ym, self.yp),
            (self.own, 0, self.ym, self.yp),
            (self.own, None, self.xo, self.xo),
            (self.own, None, None, self.own),
            (self.ym, 0, self.yp, self.y2),
            (self.yp, 1, self.ym, self.y2),
            (self.xo, None, self.yp, self.xm),
            (self.xo, None, self.ym, self.xp),
            (self.y2, 0, self.xo, self.x2),
            (self.y2, 1, self.xo, self.x2),
            (self.ym, None, None, self.ym),
            (self.yp, None, None, self.yp),
            (self.xo, None, None, self.xo),
            (self.y2, None, None, self.y2),
            (self.xm, None, None, self.xm),
            (self.xp, None, None, self.xp),
            (self.x2, None, None, self.x2),
        ]
        self.near = [(v // 2, slot) for v, slot in ((self.own, 5), (self.xo, 14), (self.ym, 12), (self.yp, 13))]
        self.later = [(v // 2, slot) for v, slot in ((self.y2, 15), (self.xm, 16), (self.xp, 17), (self.x2, 18))]

    def copy(self, slot, received):
        sent, half, target, incoming = self.table[slot]
        if target is None:
            target = self.own + self.flip
            incoming = incoming + self.flip
        block = incoming if received else sent
        ref = self.buf.at[block]
        if half is not None:
            ref = self.buf.at[block, pl.ds(half * HALF, HALF)]
        return remote(ref, ref, self.ss, self.rs.at[slot], {"dp": target})

    def send(self, *slots):
        for slot in slots:
            self.copy(slot, False).start()

    def recv(self, *slots):
        for slot in slots:
            self.copy(slot, True).wait_recv()

    def stage_a(self):
        self.send(0, 2, 1, 3, 4, 5)

    def stage_b(self):
        self.recv(0)
        self.send(6)
        self.recv(2)
        self.send(7)
        self.recv(4)
        self.send(8, 9, 14)
        self.recv(1)
        self.send(12)
        self.recv(3)
        self.send(13)

    def stage_c(self):
        self.recv(6)
        self.send(10)
        self.recv(7)
        self.send(11, 15)

    def stage_d(self):
        self.recv(8)
        self.send(16)
        self.recv(9)
        self.send(17)
        self.recv(10, 11)
        self.send(18)

    def drain(self):
        every = self.buf.at[pl.ds(0, PEERS - 1)]
        remote(every, every, self.ss, self.rs.at[0], self.any_peer).wait_send()


class HiddenGather:
    def __init__(self, buf, ss, rs, feat):
        self.buf, self.ss, self.rs = buf, ss, rs
        z, xh = feat // 2, feat % 2
        self.rows = buf.shape[1] // 2

        def at(step, q):
            return ((z + 8 + step) % 8) * 2 + (xh if q == 0 else 1 - xh)

        up, down, partner = at(1, 0), at(-1, 0), at(0, 1)
        self.any_peer = {"feat": partner}
        self.table = {0: (at(0, 0), None, partner, partner)}
        for q in range(2):
            base = 1 + 8 * q
            for k in range(4):
                last = k == 3
                self.table[base + 2 * k] = (at(-k, q), 0 if last else None, up, at(-k - 1, q))
                self.table[base + 2 * k + 1] = (at(k, q), 1 if last else None, down, at(k + 1, q))

    def copy(self, slot, received):
        sent, half, target, incoming = self.table[slot]
        block = incoming if received else sent
        if half is None:
            ref = self.buf.at[block]
        else:
            ref = self.buf.at[block, pl.ds(half * self.rows, self.rows)]
        return remote(ref, ref, self.ss, self.rs.at[slot], {"feat": target})

    def send(self, *slots):
        for slot in slots:
            self.copy(slot, False).start()

    def recv(self, *slots):
        for slot in slots:
            self.copy(slot, True).wait_recv()

    def step(self, q, k):
        base = 1 + 8 * q + 2 * k
        if k:
            self.recv(base - 2, base - 1)
        self.send(base, base + 1)

    def drain(self):
        every = self.buf.at[pl.ds(0, PEERS - 1)]
        remote(every, every, self.ss, self.rs.at[0], self.any_peer).wait_send()


def exchange(axis, me, source, target, every, ss, rs):
    def start():
        def step(j, carry):
            peer = (me + j) % PEERS
            remote(source(peer), target, ss, rs, {axis: peer}).start()
            return carry

        lax.fori_loop(1, PEERS, step, 0)

    def all_of_them():
        return remote(every, every, ss, rs, {axis: (me + 1) % PEERS})

    return start, lambda: all_of_them().wait_recv(), lambda: all_of_them().wait_send()


def fold(values):
    return jnp.sum(values.reshape(CHUNK // 8, 8, COLS), axis=0)


def over_rows(blocks, step, init):
    per = ROWS // CHUNK

    def body(i, carry):
        return step(i // per, pl.ds(pl.multiple_of((i % per) * CHUNK, CHUNK), CHUNK), carry)

    return lax.fori_loop(0, blocks * per, body, init)


def local_statistics(ref):
    zero = jnp.zeros((8, COLS), F32)

    def add(block, rows, acc):
        return acc + fold(ref[rows].astype(F32))

    mean = jnp.sum(over_rows(1, add, zero), axis=0, keepdims=True) / ROWS

    def add_square(block, rows, acc):
        off = ref[rows].astype(F32) - mean
        return acc + fold(off * off)

    return mean, jnp.sum(over_rows(1, add_square, zero), axis=0, keepdims=True)


def merge_statistics(stats, view, batch):
    zero = jnp.zeros((1, COLS), F32)
    centre = lax.fori_loop(
        0, PEERS, lambda j, acc: acc + stats[view, j, 0:1], zero
    ) / PEERS

    def add(j, acc):
        off = stats[view, j, 0:1] - centre
        return acc + (stats[view, j, 1:2] + off * off * ROWS)

    spread = lax.fori_loop(0, PEERS, add, zero) / batch
    return centre, lax.rsqrt(spread + eps)


def kernel(
    packed, scale_ref, grad_acc,
    weight, loss_ref,
    one, two, grad, hid, normed_one, normed_two, fixed, raw, part, part_in, gram, spread, stats, sums, losses, length, mirror,
    local_sem, one_s, one_r, two_s, two_r, grad_s, grad_r, hid_s, hid_r,
    part_s, part_r, gram_s, gram_r, stats_s, stats_r, sums_s, sums_r, loss_s, loss_r, mirror_s, mirror_r,
):
    dp, feat = lax.axis_index("dp"), lax.axis_index("feat")
    batch = ROWS * PEERS
    width = COLS * PEERS

    local = [
        pltpu.make_async_copy(packed.at[0], two.at[dp], local_sem.at[0]),
        pltpu.make_async_copy(packed.at[1], one.at[dp], local_sem.at[1]),
        pltpu.make_async_copy(packed.at[2], raw, local_sem.at[2]),
    ]
    base = pltpu.make_async_copy(grad_acc, weight, local_sem.at[3])
    base.start()
    for copy in local:
        copy.start()

    barrier = pltpu.get_barrier_semaphore()

    def greet(j, carry):
        pl.semaphore_signal(
            barrier, inc=1, device_id={"dp": (dp + j) % PEERS}, device_id_type=MESH
        )
        pl.semaphore_signal(
            barrier, inc=1, device_id={"feat": (feat + j) % PEERS}, device_id_type=MESH
        )
        return carry

    lax.fori_loop(1, PEERS, greet, 0)
    for copy in local:
        copy.wait()

    gather_two = DpGather(two, two_s, two_r, dp)
    gather_one = DpGather(one, one_s, one_r, dp)
    gather_grad = DpGather(grad, grad_s, grad_r, dp)
    gather_hid = HiddenGather(hid, hid_s, hid_r, feat)
    stats_moves = [
        exchange(
            "dp", dp, lambda p, k=k: stats.at[k, dp], stats.at[k, dp],
            stats.at[k, pl.ds(0, PEERS - 1)], stats_s.at[k], stats_r.at[k],
        )
        for k in range(2)
    ]
    def piece(k, owner):
        return pl.ds(pl.multiple_of(owner * PIECE[k], 16), PIECE[k])

    part_moves = [
        exchange(
            "feat", feat, lambda p, k=k: part.at[k, piece(k, p)],
            part_in.at[k, feat, pl.ds(0, PIECE[k])],
            part_in.at[k, pl.ds(0, PEERS - 1), pl.ds(0, PIECE[k])], part_s.at[k], part_r.at[k],
        )
        for k in range(2)
    ]
    gram_moves = [
        exchange(
            "feat", feat, lambda p, k=k: gram.at[k, piece(k, feat)], gram.at[k, piece(k, feat)],
            gram.at[k, pl.ds(0, (PEERS - 1) * PIECE[k])], gram_s.at[k], gram_r.at[k],
        )
        for k in range(2)
    ]
    pl.semaphore_wait(barrier, 2 * (PEERS - 1))

    gather_two.stage_a()

    def start_statistics(view, buf):
        mean, square = local_statistics(buf.at[dp])
        stats[view, dp, 0:1] = mean
        stats[view, dp, 1:2] = square
        stats_moves[view][0]()

    start_statistics(0, two)
    hid[feat] = raw[...].T
    gather_hid.send(0)
    gather_hid.step(0, 0)
    gather_two.stage_b()
    gather_hid.step(0, 1)
    stats_moves[0][1]()
    centre, inverse = merge_statistics(stats, 0, batch)

    def norm_two(pair):
        def norm(block, rows, carry):
            values = two[2 * pair + block, rows].astype(F32)
            normed_two[2 * pair + block, rows] = ((values - centre) * inverse).astype(BF)
            return carry

        over_rows(2, norm, 0)

    def gram_tiles(group, place, first, count):
        tile = lax.dot_general(
            normed_two[dp],
            normed_two[pl.ds(first, count)].reshape(count * ROWS, COLS),
            (((1,), (1,)), ((), ())),
            preferred_element_type=F32,
        ).astype(BF)
        for k in range(count):
            rows = pl.ds((place + k) * ROWS, ROWS)
            part[group, rows] = tile[:, k * ROWS : (k + 1) * ROWS]

    def add_parts(group):
        size = PIECE[group]
        part_in[group, feat, :size] = part[group, piece(group, feat)]
        part_moves[group][1]()

        def add(j, acc):
            return acc + part_in[group, j, :size].astype(F32)

        total = lax.fori_loop(0, PEERS, add, jnp.zeros((size, ROWS), F32))
        gram[group, piece(group, feat)] = total.astype(BF)
        gram_moves[group][0]()

    core, y, x = dp % 2, (dp // 2) % 4, dp // 8
    by_x = jnp.where(x == 0, core, 1 - core)
    by_y = jnp.where(y < 2, core, 1 - core)
    pair_of = {
        name: getattr(gather_two, name) // 2 for name in ("own", "xo", "ym", "yp", "y2", "xm", "xp", "x2")
    }
    xo_block, y2_block, x2_block = (
        2 * pair_of[name] + kept for name, kept in (("xo", by_x), ("y2", by_y), ("x2", by_x))
    )

    def mirror_copy(group, place, target, slot):
        return remote(
            gram.at[group, pl.ds(place * ROWS, ROWS)],
            mirror.at[group, slot],
            mirror_s.at[group],
            mirror_r.at[group],
            {"dp": target},
        )

    mirror_sends = (
        [(2, xo_block, 2), (3, 2 * pair_of["ym"], core), (4, 2 * pair_of["ym"] + 1, core)],
        [
            (0, y2_block, 2),
            (1, 2 * pair_of["xm"], core),
            (2, 2 * pair_of["xm"] + 1, core),
            (3, x2_block, 3),
        ],
    )

    def mirror_start(group):
        for place, target, slot in mirror_sends[group]:
            mirror_copy(group, place, target, slot).start()

    def mirror_all(group):
        every = mirror.at[group, pl.ds(0, len(mirror_sends[group]))]
        return remote(every, every, mirror_s.at[group], mirror_r.at[group], {"dp": xo_block})

    part[0, 5 * ROWS :] = jnp.zeros((ROWS, ROWS), BF)
    gather_two.recv(5)
    norm_two(pair_of["own"])
    gram_tiles(0, 0, 2 * pair_of["own"], 2)
    gather_two.recv(14)
    norm_two(pair_of["xo"])
    gram_tiles(0, 2, xo_block, 1)
    gather_two.recv(12)
    norm_two(pair_of["ym"])
    gram_tiles(0, 3, 2 * pair_of["ym"], 2)
    part_moves[0][0]()
    gather_two.stage_c()
    gather_hid.recv(0)
    gather_hid.step(1, 0)
    gather_two.recv(13)
    norm_two(pair_of["yp"])
    gather_two.recv(15)
    norm_two(pair_of["y2"])
    gram_tiles(1, 0, y2_block, 1)
    gather_two.stage_d()
    gather_one.stage_a()
    gather_two.recv(16)
    norm_two(pair_of["xm"])
    gram_tiles(1, 1, 2 * pair_of["xm"], 2)
    gather_two.recv(18)
    norm_two(pair_of["x2"])
    gram_tiles(1, 3, x2_block, 1)
    part_moves[1][0]()
    gather_two.recv(17)
    norm_two(pair_of["xp"])
    start_statistics(1, one)
    add_parts(0)
    gather_hid.step(0, 2)
    gather_one.stage_b()
    stats_moves[1][1]()
    centre_one, inverse_one = merge_statistics(stats, 1, batch)

    def norm_pair(pair, acc):
        for block in range(2):
            at = 2 * pair + block

            def norm(i, rows, accs):
                values = one[at, rows].astype(F32)
                normed = ((values - centre_one) * inverse_one).astype(BF)
                normed_one[at, rows] = normed
                share = normed.astype(F32)
                return (
                    accs[0] + fold(share * normed_two[at, rows].astype(F32)),
                    accs[1] + fold(share * share),
                )

            acc, norms = over_rows(1, norm, (acc, jnp.zeros((8, COLS), F32)))
            norms = jnp.sum(norms, axis=0, keepdims=True)
            length[at] = 1.0 / jnp.maximum(norms, 1e-3)
        return acc

    acc = jnp.zeros((8, COLS), F32)
    gather_one.stage_c()
    for pair, slot in gather_one.near:
        gather_one.recv(slot)
        acc = norm_pair(pair, acc)
    add_parts(1)
    gram_moves[0][1]()
    mirror_start(0)
    gather_hid.step(1, 1)
    gather_one.stage_d()
    gather_hid.step(0, 3)
    for pair, slot in gather_one.later:
        gather_one.recv(slot)
        acc = norm_pair(pair, acc)
    corr = jnp.sum(acc, axis=0, keepdims=True) / batch
    scale = scale_ref[0] / batch
    weight_diag = scale * (-2.0 * (1.0 - corr) - 2.0 * off_weight * corr)

    def add_spread(group, terms):
        for k in range(0, len(terms), 2):
            some = terms[k : k + 2]
            product = jnp.dot(
                jnp.concatenate([tile for tile, _ in some], axis=1),
                jnp.concatenate([normed_one[block] for _, block in some], axis=0),
                preferred_element_type=F32,
            )
            if group == 0 and k == 0:
                spread[...] = product
            else:
                spread[...] += product

    def kept_tile(group, place):
        return gram[group, place * ROWS : (place + 1) * ROWS]

    def mirrored_tile(group, slot):
        return mirror[group, slot].T

    gram_moves[1][1]()
    mirror_start(1)
    mirror_all(0).wait_recv()
    add_spread(
        0,
        [
            (kept_tile(0, 0), 2 * pair_of["own"]),
            (kept_tile(0, 1), 2 * pair_of["own"] + 1),
            (kept_tile(0, 2), xo_block),
            (mirrored_tile(0, 2), 4 * pair_of["xo"] + 1 - xo_block),
            (kept_tile(0, 3), 2 * pair_of["ym"]),
            (kept_tile(0, 4), 2 * pair_of["ym"] + 1),
            (mirrored_tile(0, 0), 2 * pair_of["yp"]),
            (mirrored_tile(0, 1), 2 * pair_of["yp"] + 1),
        ],
    )
    gather_hid.step(1, 2)
    mirror_all(1).wait_recv()
    add_spread(
        1,
        [
            (kept_tile(1, 0), y2_block),
            (mirrored_tile(1, 2), 4 * pair_of["y2"] + 1 - y2_block),
            (kept_tile(1, 1), 2 * pair_of["xm"]),
            (kept_tile(1, 2), 2 * pair_of["xm"] + 1),
            (mirrored_tile(1, 0), 2 * pair_of["xp"]),
            (mirrored_tile(1, 1), 2 * pair_of["xp"] + 1),
            (kept_tile(1, 3), x2_block),
            (mirrored_tile(1, 3), 4 * pair_of["x2"] + 1 - x2_block),
        ],
    )
    factor = scale * (2.0 * off_weight / batch)
    zero = jnp.zeros((8, COLS), F32)

    def norm_step(block, rows, accs):
        raw_spread = spread[rows]
        share = normed_one[dp, rows].astype(F32)
        value = raw_spread * factor + normed_two[dp, rows].astype(F32) * weight_diag
        spread[rows] = value
        return (
            accs[0] + fold(value),
            accs[1] + fold(value * share),
            accs[2] + fold(raw_spread * share),
        )

    accs = over_rows(1, norm_step, (zero, zero, zero))
    sum_grad = jnp.sum(accs[0], axis=0, keepdims=True)
    sum_cross = jnp.sum(accs[1], axis=0, keepdims=True)
    near_tilt = sum_cross * length[dp]

    def grad_step(block, rows, carry):
        share = normed_one[dp, rows].astype(F32)
        grad[dp, rows] = (spread[rows] - share * near_tilt).astype(BF)
        return carry

    over_rows(1, grad_step, 0)
    gather_grad.stage_a()
    gather_hid.step(1, 3)
    square = jnp.sum(accs[2], axis=0, keepdims=True) / (float(batch) * float(batch))
    terms = off_weight * square + (
        (1.0 - corr) * (1.0 - corr) - off_weight * corr * corr
    ) * (1.0 / PEERS)
    lanes = terms[:, :128]
    for k in range(1, COLS // 128):
        lanes = lanes + terms[:, k * 128 : (k + 1) * 128]
    sums[dp, 0:1, :COLS] = sum_grad
    sums[dp, 1:2, :COLS] = sum_cross
    sums[dp, 0:1, COLS:] = lanes
    sums[dp, 1:2, COLS:] = jnp.zeros_like(lanes)
    sums_start, sums_recv, sums_send = exchange(
        "dp", dp, lambda p: sums.at[dp], sums.at[dp], sums.at[pl.ds(0, PEERS - 1)], sums_s, sums_r
    )
    sums_start()
    gather_grad.stage_b()
    gather_grad.stage_c()
    sums_recv()
    total = lax.fori_loop(
        0, PEERS, lambda j, acc: acc + sums[j], jnp.zeros((2, COLS + 128), F32)
    )
    losses[feat] = total[:, COLS:]
    loss_start, loss_recv, loss_send = exchange(
        "feat", feat, lambda p: losses.at[feat], losses.at[feat],
        losses.at[pl.ds(0, PEERS - 1)], loss_s, loss_r,
    )
    loss_start()
    mean_grad = total[0:1, :COLS] / batch
    mean_cross = total[1:2, :COLS] / batch

    def fix_pair(pair, place):
        for block in range(2):
            at = 2 * pair + block
            tilt = mean_cross - sums[at, 1:2, :COLS] * length[at]

            def fix(i, rows, carry):
                share = normed_one[at, rows].astype(F32)
                value = grad[at, rows].astype(F32) - mean_grad - share * tilt
                fixed[2 * place + block, rows] = (value * inverse_one).astype(BF)
                return carry

            over_rows(1, fix, 0)

    def add_pairs(pairs, first):
        count = 2 * len(pairs)

        def step(i, carry):
            rows = pl.ds(pl.multiple_of(i * 1024, 1024), 1024)
            lhs = jnp.concatenate(
                [hid[2 * pair + block, rows] for pair in pairs for block in range(2)], axis=1
            )
            product = jnp.dot(
                lhs, fixed[:count].reshape(count * ROWS, COLS), preferred_element_type=F32
            )
            if first:
                weight[rows] += product
            else:
                weight[rows] += product
            return carry

        lax.fori_loop(0, COLS // 1024, step, 0)

    def finish_pairs(group, first):
        for place, (pair, slot) in enumerate(group):
            gather_grad.recv(slot)
            fix_pair(pair, place)
        add_pairs([pair for pair, _ in group], first)

    gather_hid.recv(7, 8, 15, 16)
    base.wait()
    finish_pairs(gather_grad.near[:2], True)
    finish_pairs(gather_grad.near[2:], False)
    finish_pairs(gather_grad.later[:1], False)
    gather_grad.stage_d()
    finish_pairs(gather_grad.later[1:], False)

    loss_recv()
    all_loss = lax.fori_loop(
        0, PEERS, lambda j, acc: acc + losses[j], jnp.zeros((2, 128), F32)
    )
    loss_ref[0] = jnp.sum(all_loss) / width
    gather_two.drain()
    gather_one.drain()
    gather_grad.drain()
    gather_hid.drain()
    for group in range(2):
        stats_moves[group][2]()
        part_moves[group][2]()
        gram_moves[group][2]()
        mirror_all(group).wait_send()
    sums_send()
    loss_send()


def body(z_one, z_two, hidden_in, grad_acc, loss_scale):
    in_hbm = pl.BlockSpec(memory_space=pltpu.HBM)
    in_smem = pl.BlockSpec(memory_space=pltpu.SMEM)
    dma = pltpu.SemaphoreType.DMA
    weight_grad, loss = pl.pallas_call(
        kernel,
        out_shape=(
            jax.ShapeDtypeStruct((COLS, COLS), F32),
            jax.ShapeDtypeStruct((1,), F32),
        ),
        in_specs=[in_hbm, in_smem, in_hbm],
        out_specs=(pl.BlockSpec(memory_space=pltpu.VMEM), in_smem),
        scratch_shapes=[
            pltpu.VMEM((PEERS, ROWS, COLS), BF),
            pltpu.VMEM((PEERS, ROWS, COLS), BF),
            pltpu.VMEM((PEERS, ROWS, COLS), BF),
            pltpu.VMEM((PEERS, COLS, ROWS), BF),
            pltpu.VMEM((PEERS, ROWS, COLS), BF),
            pltpu.VMEM((PEERS, ROWS, COLS), BF),
            pltpu.VMEM((6, ROWS, COLS), BF),
            pltpu.VMEM((ROWS, COLS), BF),
            pltpu.VMEM((2, 6 * ROWS, ROWS), BF),
            pltpu.VMEM((2, PEERS, PIECE[0], ROWS), BF),
            pltpu.VMEM((2, 6 * ROWS, ROWS), BF),
            pltpu.VMEM((ROWS, COLS), F32),
            pltpu.VMEM((2, PEERS, 2, COLS), F32),
            pltpu.VMEM((PEERS, 2, COLS + 128), F32),
            pltpu.VMEM((PEERS, 2, 128), F32),
            pltpu.VMEM((PEERS, 1, COLS), F32),
            pltpu.VMEM((2, 4, ROWS, ROWS), BF),
            dma((4,)),
        ]
        + [dma, dma((19,))] * 3
        + [dma, dma((17,))]
        + [dma((2,))] * 6
        + [dma] * 4
        + [dma((2,))] * 2,
        compiler_params=pltpu.CompilerParams(
            collective_id=0, has_side_effects=True, vmem_limit_bytes=48 << 20
        ),
        cost_estimate=pl.CostEstimate(
            flops=6 * 10**9, bytes_accessed=8 * 10**6, transcendentals=0
        ),
        name="barlow",
    )(jnp.stack([z_two, z_one, hidden_in]), loss_scale, grad_acc)
    return weight_grad, loss


def solution(mesh):
    placed = (P("dp", "feat"), P("dp", "feat"), P("feat", "dp"), P("dp", "feat"), P())
    return jax.shard_map(
        body, mesh=mesh, in_specs=placed, out_specs=(P("dp", "feat"), P()), check_vma=False
    )
```

```python
import jax
import jax.numpy as jnp
from jax import lax
from jax.experimental import pallas as pl
from jax.experimental.pallas import tpu as pltpu
from jax.sharding import PartitionSpec as P

MESH = pl.DeviceIdType.MESH
BF = jnp.bfloat16
F32 = jnp.float32
off_weight = 0.0051
eps = 1e-05
PEERS = 16
ROWS = 128
COLS = 1024
HALF = ROWS // 2
PIECE = (48, 32)
CHUNK = 64


def remote(src, dst, ss, rs, device):
    return pltpu.make_async_remote_copy(
        src_ref=src, dst_ref=dst, send_sem=ss, recv_sem=rs, device_id=device, device_id_type=MESH
    )


class DpGather:
    def __init__(self, buf, ss, rs, dp):
        self.buf, self.ss, self.rs = buf, ss, rs
        core, y, x = dp % 2, (dp // 2) % 4, dp // 8

        def block(x_, y_):
            return (x_ * 4 + y_) * 2 + core

        low, high, far = (y + 3) % 4, (y + 1) % 4, (y + 2) % 4
        self.own, self.ym, self.yp, self.y2 = (block(x, v) for v in (y, low, high, far))
        self.xo, self.xm, self.xp, self.x2 = (block(1 - x, v) for v in (y, low, high, far))
        self.flip = 1 - 2 * core
        self.any_peer = {"dp": self.xo}
        self.table = [
            (self.own, 0, self.yp, self.ym),
            (self.own, 1, self.yp, self.ym),
            (self.own, 1, self.ym, self.yp),
            (self.own, 0, self.ym, self.yp),
            (self.own, None, self.xo, self.xo),
            (self.own, None, None, self.own),
            (self.ym, 0, self.yp, self.y2),
            (self.yp, 1, self.ym, self.y2),
            (self.xo, None, self.yp, self.xm),
            (self.xo, None, self.ym, self.xp),
            (self.y2, 0, self.xo, self.x2),
            (self.y2, 1, self.xo, self.x2),
            (self.ym, None, None, self.ym),
            (self.yp, None, None, self.yp),
            (self.xo, None, None, self.xo),
            (self.y2, None, None, self.y2),
            (self.xm, None, None, self.xm),
            (self.xp, None, None, self.xp),
            (self.x2, None, None, self.x2),
        ]
        self.near = [(v // 2, slot) for v, slot in ((self.own, 5), (self.xo, 14), (self.ym, 12), (self.yp, 13))]
        self.later = [(v // 2, slot) for v, slot in ((self.y2, 15), (self.xm, 16), (self.xp, 17), (self.x2, 18))]

    def copy(self, slot, received):
        sent, half, target, incoming = self.table[slot]
        if target is None:
            target = self.own + self.flip
            incoming = incoming + self.flip
        block = incoming if received else sent
        ref = self.buf.at[block]
        if half is not None:
            ref = self.buf.at[block, pl.ds(half * HALF, HALF)]
        return remote(ref, ref, self.ss, self.rs.at[slot], {"dp": target})

    def send(self, *slots):
        for slot in slots:
            self.copy(slot, False).start()

    def recv(self, *slots):
        for slot in slots:
            self.copy(slot, True).wait_recv()

    def stage_a(self):
        self.send(0, 2, 1, 3, 4, 5)

    def stage_b(self):
        self.recv(0)
        self.send(6)
        self.recv(2)
        self.send(7)
        self.recv(4)
        self.send(8, 9, 14)
        self.recv(1)
        self.send(12)
        self.recv(3)
        self.send(13)

    def stage_c(self):
        self.recv(6)
        self.send(10)
        self.recv(7)
        self.send(11, 15)

    def stage_d(self):
        self.recv(8)
        self.send(16)
        self.recv(9)
        self.send(17)
        self.recv(10, 11)
        self.send(18)

    def drain(self):
        every = self.buf.at[pl.ds(0, PEERS - 1)]
        remote(every, every, self.ss, self.rs.at[0], self.any_peer).wait_send()


class HiddenGather:
    def __init__(self, buf, ss, rs, feat):
        self.buf, self.ss, self.rs = buf, ss, rs
        z, xh = feat // 2, feat % 2
        self.rows = buf.shape[1] // 2

        def at(step, q):
            return ((z + 8 + step) % 8) * 2 + (xh if q == 0 else 1 - xh)

        up, down, partner = at(1, 0), at(-1, 0), at(0, 1)
        self.any_peer = {"feat": partner}
        self.table = {0: (at(0, 0), None, partner, partner)}
        for q in range(2):
            base = 1 + 8 * q
            for k in range(4):
                last = k == 3
                self.table[base + 2 * k] = (at(-k, q), 0 if last else None, up, at(-k - 1, q))
                self.table[base + 2 * k + 1] = (at(k, q), 1 if last else None, down, at(k + 1, q))

    def copy(self, slot, received):
        sent, half, target, incoming = self.table[slot]
        block = incoming if received else sent
        if half is None:
            ref = self.buf.at[block]
        else:
            ref = self.buf.at[block, pl.ds(half * self.rows, self.rows)]
        return remote(ref, ref, self.ss, self.rs.at[slot], {"feat": target})

    def send(self, *slots):
        for slot in slots:
            self.copy(slot, False).start()

    def recv(self, *slots):
        for slot in slots:
            self.copy(slot, True).wait_recv()

    def step(self, q, k):
        base = 1 + 8 * q + 2 * k
        if k:
            self.recv(base - 2, base - 1)
        self.send(base, base + 1)

    def drain(self):
        every = self.buf.at[pl.ds(0, PEERS - 1)]
        remote(every, every, self.ss, self.rs.at[0], self.any_peer).wait_send()


def exchange(axis, me, source, target, every, ss, rs):
    def start():
        def step(j, carry):
            peer = (me + j) % PEERS
            remote(source(peer), target, ss, rs, {axis: peer}).start()
            return carry

        lax.fori_loop(1, PEERS, step, 0)

    def all_of_them():
        return remote(every, every, ss, rs, {axis: (me + 1) % PEERS})

    return start, lambda: all_of_them().wait_recv(), lambda: all_of_them().wait_send()


def fold(values):
    return jnp.sum(values.reshape(CHUNK // 8, 8, COLS), axis=0)


def over_rows(blocks, step, init):
    per = ROWS // CHUNK

    def body(i, carry):
        return step(i // per, pl.ds(pl.multiple_of((i % per) * CHUNK, CHUNK), CHUNK), carry)

    return lax.fori_loop(0, blocks * per, body, init)


def local_statistics(ref):
    zero = jnp.zeros((8, COLS), F32)

    def add(block, rows, acc):
        return acc + fold(ref[rows].astype(F32))

    mean = jnp.sum(over_rows(1, add, zero), axis=0, keepdims=True) / ROWS

    def add_square(block, rows, acc):
        off = ref[rows].astype(F32) - mean
        return acc + fold(off * off)

    return mean, jnp.sum(over_rows(1, add_square, zero), axis=0, keepdims=True)


def merge_statistics(stats, view, batch):
    zero = jnp.zeros((1, COLS), F32)
    centre = lax.fori_loop(
        0, PEERS, lambda j, acc: acc + stats[view, j, 0:1], zero
    ) / PEERS

    def add(j, acc):
        off = stats[view, j, 0:1] - centre
        return acc + (stats[view, j, 1:2] + off * off * ROWS)

    spread = lax.fori_loop(0, PEERS, add, zero) / batch
    return centre, lax.rsqrt(spread + eps)


def kernel(
    z_two, z_one, hidden, scale_ref, grad_acc,
    weight, loss_ref,
    one, two, grad, hid, normed_one, normed_two, fixed, raw, part, part_in, gram, spread, stats, sums, losses, length, mirror,
    local_sem, one_s, one_r, two_s, two_r, grad_s, grad_r, hid_s, hid_r,
    part_s, part_r, gram_s, gram_r, stats_s, stats_r, sums_s, sums_r, loss_s, loss_r, mirror_s, mirror_r,
):
    dp, feat = lax.axis_index("dp"), lax.axis_index("feat")
    batch = ROWS * PEERS
    width = COLS * PEERS

    local = [
        pltpu.make_async_copy(z_two, two.at[dp], local_sem.at[0]),
        pltpu.make_async_copy(z_one, one.at[dp], local_sem.at[1]),
        pltpu.make_async_copy(hidden, raw, local_sem.at[2]),
    ]
    base = pltpu.make_async_copy(grad_acc, weight, local_sem.at[3])
    base.start()
    for copy in local:
        copy.start()

    barrier = pltpu.get_barrier_semaphore()

    def greet(j, carry):
        pl.semaphore_signal(
            barrier, inc=1, device_id={"dp": (dp + j) % PEERS}, device_id_type=MESH
        )
        pl.semaphore_signal(
            barrier, inc=1, device_id={"feat": (feat + j) % PEERS}, device_id_type=MESH
        )
        return carry

    lax.fori_loop(1, PEERS, greet, 0)
    for copy in local:
        copy.wait()

    gather_two = DpGather(two, two_s, two_r, dp)
    gather_one = DpGather(one, one_s, one_r, dp)
    gather_grad = DpGather(grad, grad_s, grad_r, dp)
    gather_hid = HiddenGather(hid, hid_s, hid_r, feat)
    stats_moves = [
        exchange(
            "dp", dp, lambda p, k=k: stats.at[k, dp], stats.at[k, dp],
            stats.at[k, pl.ds(0, PEERS - 1)], stats_s.at[k], stats_r.at[k],
        )
        for k in range(2)
    ]
    def piece(k, owner):
        return pl.ds(pl.multiple_of(owner * PIECE[k], 16), PIECE[k])

    part_moves = [
        exchange(
            "feat", feat, lambda p, k=k: part.at[k, piece(k, p)],
            part_in.at[k, feat, pl.ds(0, PIECE[k])],
            part_in.at[k, pl.ds(0, PEERS - 1), pl.ds(0, PIECE[k])], part_s.at[k], part_r.at[k],
        )
        for k in range(2)
    ]
    gram_moves = [
        exchange(
            "feat", feat, lambda p, k=k: gram.at[k, piece(k, feat)], gram.at[k, piece(k, feat)],
            gram.at[k, pl.ds(0, (PEERS - 1) * PIECE[k])], gram_s.at[k], gram_r.at[k],
        )
        for k in range(2)
    ]
    pl.semaphore_wait(barrier, 2 * (PEERS - 1))

    gather_two.stage_a()

    def start_statistics(view, buf):
        mean, square = local_statistics(buf.at[dp])
        stats[view, dp, 0:1] = mean
        stats[view, dp, 1:2] = square
        stats_moves[view][0]()

    start_statistics(0, two)
    hid[feat] = raw[...].T
    gather_hid.send(0)
    gather_hid.step(0, 0)
    gather_two.stage_b()
    gather_hid.step(0, 1)
    stats_moves[0][1]()
    centre, inverse = merge_statistics(stats, 0, batch)

    def norm_two(pair):
        def norm(block, rows, carry):
            values = two[2 * pair + block, rows].astype(F32)
            normed_two[2 * pair + block, rows] = ((values - centre) * inverse).astype(BF)
            return carry

        over_rows(2, norm, 0)

    def gram_tiles(group, place, first, count):
        tile = lax.dot_general(
            normed_two[dp],
            normed_two[pl.ds(first, count)].reshape(count * ROWS, COLS),
            (((1,), (1,)), ((), ())),
            preferred_element_type=F32,
        ).astype(BF)
        for k in range(count):
            rows = pl.ds((place + k) * ROWS, ROWS)
            part[group, rows] = tile[:, k * ROWS : (k + 1) * ROWS]

    def add_parts(group):
        size = PIECE[group]
        part_in[group, feat, :size] = part[group, piece(group, feat)]
        part_moves[group][1]()

        def add(j, acc):
            return acc + part_in[group, j, :size].astype(F32)

        total = lax.fori_loop(0, PEERS, add, jnp.zeros((size, ROWS), F32))
        gram[group, piece(group, feat)] = total.astype(BF)
        gram_moves[group][0]()

    core, y, x = dp % 2, (dp // 2) % 4, dp // 8
    by_x = jnp.where(x == 0, core, 1 - core)
    by_y = jnp.where(y < 2, core, 1 - core)
    pair_of = {
        name: getattr(gather_two, name) // 2 for name in ("own", "xo", "ym", "yp", "y2", "xm", "xp", "x2")
    }
    xo_block, y2_block, x2_block = (
        2 * pair_of[name] + kept for name, kept in (("xo", by_x), ("y2", by_y), ("x2", by_x))
    )

    def mirror_copy(group, place, target, slot):
        return remote(
            gram.at[group, pl.ds(place * ROWS, ROWS)],
            mirror.at[group, slot],
            mirror_s.at[group],
            mirror_r.at[group],
            {"dp": target},
        )

    mirror_sends = (
        [(2, xo_block, 2), (3, 2 * pair_of["ym"], core), (4, 2 * pair_of["ym"] + 1, core)],
        [
            (0, y2_block, 2),
            (1, 2 * pair_of["xm"], core),
            (2, 2 * pair_of["xm"] + 1, core),
            (3, x2_block, 3),
        ],
    )

    def mirror_start(group):
        for place, target, slot in mirror_sends[group]:
            mirror_copy(group, place, target, slot).start()

    def mirror_all(group):
        every = mirror.at[group, pl.ds(0, len(mirror_sends[group]))]
        return remote(every, every, mirror_s.at[group], mirror_r.at[group], {"dp": xo_block})

    part[0, 5 * ROWS :] = jnp.zeros((ROWS, ROWS), BF)
    gather_two.recv(5)
    norm_two(pair_of["own"])
    gram_tiles(0, 0, 2 * pair_of["own"], 2)
    gather_two.recv(14)
    norm_two(pair_of["xo"])
    gram_tiles(0, 2, xo_block, 1)
    gather_two.recv(12)
    norm_two(pair_of["ym"])
    gram_tiles(0, 3, 2 * pair_of["ym"], 2)
    part_moves[0][0]()
    gather_two.stage_c()
    gather_hid.recv(0)
    gather_hid.step(1, 0)
    gather_two.recv(13)
    norm_two(pair_of["yp"])
    gather_two.recv(15)
    norm_two(pair_of["y2"])
    gram_tiles(1, 0, y2_block, 1)
    gather_two.stage_d()
    gather_one.stage_a()
    gather_two.recv(16)
    norm_two(pair_of["xm"])
    gram_tiles(1, 1, 2 * pair_of["xm"], 2)
    gather_two.recv(18)
    norm_two(pair_of["x2"])
    gram_tiles(1, 3, x2_block, 1)
    part_moves[1][0]()
    gather_two.recv(17)
    norm_two(pair_of["xp"])
    start_statistics(1, one)
    add_parts(0)
    gather_hid.step(0, 2)
    gather_one.stage_b()
    stats_moves[1][1]()
    centre_one, inverse_one = merge_statistics(stats, 1, batch)

    def norm_pair(pair, acc):
        for block in range(2):
            at = 2 * pair + block

            def norm(i, rows, accs):
                values = one[at, rows].astype(F32)
                normed = ((values - centre_one) * inverse_one).astype(BF)
                normed_one[at, rows] = normed
                share = normed.astype(F32)
                return (
                    accs[0] + fold(share * normed_two[at, rows].astype(F32)),
                    accs[1] + fold(share * share),
                )

            acc, norms = over_rows(1, norm, (acc, jnp.zeros((8, COLS), F32)))
            norms = jnp.sum(norms, axis=0, keepdims=True)
            length[at] = 1.0 / jnp.maximum(norms, 1e-3)
        return acc

    acc = jnp.zeros((8, COLS), F32)
    gather_one.stage_c()
    for pair, slot in gather_one.near:
        gather_one.recv(slot)
        acc = norm_pair(pair, acc)
    add_parts(1)
    gram_moves[0][1]()
    mirror_start(0)
    gather_hid.step(1, 1)
    gather_one.stage_d()
    gather_hid.step(0, 3)
    for pair, slot in gather_one.later:
        gather_one.recv(slot)
        acc = norm_pair(pair, acc)
    corr = jnp.sum(acc, axis=0, keepdims=True) / batch
    scale = scale_ref[0] / batch
    weight_diag = scale * (-2.0 * (1.0 - corr) - 2.0 * off_weight * corr)

    def add_spread(group, terms):
        for k in range(0, len(terms), 2):
            some = terms[k : k + 2]
            product = jnp.dot(
                jnp.concatenate([tile for tile, _ in some], axis=1),
                jnp.concatenate([normed_one[block] for _, block in some], axis=0),
                preferred_element_type=F32,
            )
            if group == 0 and k == 0:
                spread[...] = product
            else:
                spread[...] += product

    def kept_tile(group, place):
        return gram[group, place * ROWS : (place + 1) * ROWS]

    def mirrored_tile(group, slot):
        return mirror[group, slot].T

    gram_moves[1][1]()
    mirror_start(1)
    mirror_all(0).wait_recv()
    add_spread(
        0,
        [
            (kept_tile(0, 0), 2 * pair_of["own"]),
            (kept_tile(0, 1), 2 * pair_of["own"] + 1),
            (kept_tile(0, 2), xo_block),
            (mirrored_tile(0, 2), 4 * pair_of["xo"] + 1 - xo_block),
            (kept_tile(0, 3), 2 * pair_of["ym"]),
            (kept_tile(0, 4), 2 * pair_of["ym"] + 1),
            (mirrored_tile(0, 0), 2 * pair_of["yp"]),
            (mirrored_tile(0, 1), 2 * pair_of["yp"] + 1),
        ],
    )
    gather_hid.step(1, 2)
    mirror_all(1).wait_recv()
    add_spread(
        1,
        [
            (kept_tile(1, 0), y2_block),
            (mirrored_tile(1, 2), 4 * pair_of["y2"] + 1 - y2_block),
            (kept_tile(1, 1), 2 * pair_of["xm"]),
            (kept_tile(1, 2), 2 * pair_of["xm"] + 1),
            (mirrored_tile(1, 0), 2 * pair_of["xp"]),
            (mirrored_tile(1, 1), 2 * pair_of["xp"] + 1),
            (kept_tile(1, 3), x2_block),
            (mirrored_tile(1, 3), 4 * pair_of["x2"] + 1 - x2_block),
        ],
    )
    factor = scale * (2.0 * off_weight / batch)
    zero = jnp.zeros((8, COLS), F32)

    def norm_step(block, rows, accs):
        raw_spread = spread[rows]
        share = normed_one[dp, rows].astype(F32)
        value = raw_spread * factor + normed_two[dp, rows].astype(F32) * weight_diag
        spread[rows] = value
        return (
            accs[0] + fold(value),
            accs[1] + fold(value * share),
            accs[2] + fold(raw_spread * share),
        )

    accs = over_rows(1, norm_step, (zero, zero, zero))
    sum_grad = jnp.sum(accs[0], axis=0, keepdims=True)
    sum_cross = jnp.sum(accs[1], axis=0, keepdims=True)
    near_tilt = sum_cross * length[dp]

    def grad_step(block, rows, carry):
        share = normed_one[dp, rows].astype(F32)
        grad[dp, rows] = (spread[rows] - share * near_tilt).astype(BF)
        return carry

    over_rows(1, grad_step, 0)
    gather_grad.stage_a()
    gather_hid.step(1, 3)
    square = jnp.sum(accs[2], axis=0, keepdims=True) / (float(batch) * float(batch))
    terms = off_weight * square + (
        (1.0 - corr) * (1.0 - corr) - off_weight * corr * corr
    ) * (1.0 / PEERS)
    lanes = terms[:, :128]
    for k in range(1, COLS // 128):
        lanes = lanes + terms[:, k * 128 : (k + 1) * 128]
    sums[dp, 0:1, :COLS] = sum_grad
    sums[dp, 1:2, :COLS] = sum_cross
    sums[dp, 0:1, COLS:] = lanes
    sums[dp, 1:2, COLS:] = jnp.zeros_like(lanes)
    sums_start, sums_recv, sums_send = exchange(
        "dp", dp, lambda p: sums.at[dp], sums.at[dp], sums.at[pl.ds(0, PEERS - 1)], sums_s, sums_r
    )
    sums_start()
    gather_grad.stage_b()
    gather_grad.stage_c()
    sums_recv()
    total = lax.fori_loop(
        0, PEERS, lambda j, acc: acc + sums[j], jnp.zeros((2, COLS + 128), F32)
    )
    losses[feat] = total[:, COLS:]
    loss_start, loss_recv, loss_send = exchange(
        "feat", feat, lambda p: losses.at[feat], losses.at[feat],
        losses.at[pl.ds(0, PEERS - 1)], loss_s, loss_r,
    )
    loss_start()
    mean_grad = total[0:1, :COLS] / batch
    mean_cross = total[1:2, :COLS] / batch

    def fix_pair(pair, place):
        for block in range(2):
            at = 2 * pair + block
            tilt = mean_cross - sums[at, 1:2, :COLS] * length[at]

            def fix(i, rows, carry):
                share = normed_one[at, rows].astype(F32)
                value = grad[at, rows].astype(F32) - mean_grad - share * tilt
                fixed[2 * place + block, rows] = (value * inverse_one).astype(BF)
                return carry

            over_rows(1, fix, 0)

    def add_pairs(pairs, first):
        count = 2 * len(pairs)

        def step(i, carry):
            rows = pl.ds(pl.multiple_of(i * 1024, 1024), 1024)
            lhs = jnp.concatenate(
                [hid[2 * pair + block, rows] for pair in pairs for block in range(2)], axis=1
            )
            product = jnp.dot(
                lhs, fixed[:count].reshape(count * ROWS, COLS), preferred_element_type=F32
            )
            if first:
                weight[rows] += product
            else:
                weight[rows] += product
            return carry

        lax.fori_loop(0, COLS // 1024, step, 0)

    def finish_pairs(group, first):
        for place, (pair, slot) in enumerate(group):
            gather_grad.recv(slot)
            fix_pair(pair, place)
        add_pairs([pair for pair, _ in group], first)

    gather_hid.recv(7, 8, 15, 16)
    base.wait()
    finish_pairs(gather_grad.near[:2], True)
    finish_pairs(gather_grad.near[2:], False)
    finish_pairs(gather_grad.later[:1], False)
    gather_grad.stage_d()
    finish_pairs(gather_grad.later[1:], False)

    loss_recv()
    all_loss = lax.fori_loop(
        0, PEERS, lambda j, acc: acc + losses[j], jnp.zeros((2, 128), F32)
    )
    loss_ref[0] = jnp.sum(all_loss) / width
    gather_two.drain()
    gather_one.drain()
    gather_grad.drain()
    gather_hid.drain()
    for group in range(2):
        stats_moves[group][2]()
        part_moves[group][2]()
        gram_moves[group][2]()
        mirror_all(group).wait_send()
    sums_send()
    loss_send()


def body(z_one, z_two, hidden_in, grad_acc, loss_scale):
    in_hbm = pl.BlockSpec(memory_space=pltpu.HBM)
    in_smem = pl.BlockSpec(memory_space=pltpu.SMEM)
    dma = pltpu.SemaphoreType.DMA
    weight_grad, loss = pl.pallas_call(
        kernel,
        out_shape=(
            jax.ShapeDtypeStruct((COLS, COLS), F32),
            jax.ShapeDtypeStruct((1,), F32),
        ),
        in_specs=[in_hbm, in_hbm, in_hbm, in_smem, in_hbm],
        out_specs=(pl.BlockSpec(memory_space=pltpu.VMEM), in_smem),
        scratch_shapes=[
            pltpu.VMEM((PEERS, ROWS, COLS), BF),
            pltpu.VMEM((PEERS, ROWS, COLS), BF),
            pltpu.VMEM((PEERS, ROWS, COLS), BF),
            pltpu.VMEM((PEERS, COLS, ROWS), BF),
            pltpu.VMEM((PEERS, ROWS, COLS), BF),
            pltpu.VMEM((PEERS, ROWS, COLS), BF),
            pltpu.VMEM((6, ROWS, COLS), BF),
            pltpu.VMEM((ROWS, COLS), BF),
            pltpu.VMEM((2, 6 * ROWS, ROWS), BF),
            pltpu.VMEM((2, PEERS, PIECE[0], ROWS), BF),
            pltpu.VMEM((2, 6 * ROWS, ROWS), BF),
            pltpu.VMEM((ROWS, COLS), F32),
            pltpu.VMEM((2, PEERS, 2, COLS), F32),
            pltpu.VMEM((PEERS, 2, COLS + 128), F32),
            pltpu.VMEM((PEERS, 2, 128), F32),
            pltpu.VMEM((PEERS, 1, COLS), F32),
            pltpu.VMEM((2, 4, ROWS, ROWS), BF),
            dma((4,)),
        ]
        + [dma, dma((19,))] * 3
        + [dma, dma((17,))]
        + [dma((2,))] * 6
        + [dma] * 4
        + [dma((2,))] * 2,
        compiler_params=pltpu.CompilerParams(
            collective_id=0, has_side_effects=True, vmem_limit_bytes=48 << 20
        ),
        cost_estimate=pl.CostEstimate(
            flops=6 * 10**9, bytes_accessed=8 * 10**6, transcendentals=0
        ),
        name="barlow",
    )(*(pltpu.with_memory_space_constraint(v, pltpu.HBM) for v in (z_two, z_one, hidden_in)), loss_scale, grad_acc)
    return weight_grad, loss


def solution(mesh):
    placed = (P("dp", "feat"), P("dp", "feat"), P("feat", "dp"), P("dp", "feat"), P())
    return jax.shard_map(
        body, mesh=mesh, in_specs=placed, out_specs=(P("dp", "feat"), P()), check_vma=False
    )
```
